32 devices in a mesh: expert: 8 (over y, x, core), rep: 4 (over z).
Axes of the slice: x: 2, y: 2, z: 4, core: 2. Of those that a mesh axis runs over, the one named last changes fastest.
Arguments:
- descriptors: bfloat16 [1024, 1024], P(('expert', 'rep')), may hold values from -6 to 6
- expert_ids: int32 [1024, 1], P(('expert', 'rep')), may hold values from 0 to 7; in each aligned block of 32 rows (0 to 31, 32 to 63, ...) at most 12 rows name the same one
- cotangent: bfloat16 [1024], P(('expert', 'rep')), may hold values from -6 to 6
- w1: bfloat16 [8, 1024, 2048], P('expert'), may hold values from -0.1875 to 0.1875
- w2: bfloat16 [8, 2048], P('expert'), may hold values from -0.59765625 to 0.59765625
Outputs:
- energies: bfloat16 [1024], P(('expert', 'rep'))
- descriptor_grad: bfloat16 [1024, 1024], P(('expert', 'rep'))
- w1_grad: bfloat16 [8, 2048, 1024], P('expert', 'rep')
- w2_grad: float32 [8, 2048], P('expert')
The draws below stay inside these ranges and needn't reach their ends.
Inputs may be any that keep to these rules, and one draw needn't show every extreme that they name: `expert_ids`: within the rows of one device (aligned blocks of 32 atoms) no expert id occurs more than 12 times, and some id occurs exactly 12 times.
All inputs are finite; a program needn't handle non-finite values.
Results may differ from the reference program's by a relative error of at most 0.022.
Values may be sent and summed in bfloat16 or wider, within the bound.
No kernel may reach another device: no remote copies, remote signals or barrier semaphores. Data moves between devices by JAX's collectives and lax.ppermute only.
A program may use at most 128 MiB of HBM per device.

```python
import math
import jax
import jax.numpy as jnp
import numpy as np
from jax import lax

D = 1024
H = 2048
CAP = 12
ROWS_DEV = 32
EXPERTS = 8
ATOMS = 1024
N_EXPERT = 8
N_REP = 4


def steps_of(own_key, shape, pieces, least, top_value):
    def one(position, shards_of):
        draws = jax.random.uniform(jax.random.fold_in(jax.random.fold_in(own_key, 6), position), (shards_of,), jnp.float32, least / len(pieces), top_value / len(pieces))
        return jnp.repeat(jnp.exp(draws), shape[position] // shards_of).reshape((-1,) + (1,) * (len(shape) - position - 1))

    factor_of = one(*pieces[0])
    for cut in pieces[1:]:
        factor_of = factor_of * one(*cut)
    return factor_of


def deal_out(own_key, own, number, rows, number_of, top, bound, slope):
    sequence = jax.random.permutation(own_key, number_of)
    heavy_load, usual = portions_of(number_of, rows * top, bound, slope, True), portions_of(number_of, rows * top, bound, slope, False)
    places = jnp.arange(number_of)

    def named(sizes, turn):
        used = int((sizes > 0).sum())
        fixed = max(1, used // 4)
        passed = fixed + (places - fixed + turn * (used - fixed)) % max(1, number_of - fixed)
        return jnp.zeros((number_of,), jnp.int32).at[sequence[jnp.where(places < fixed, places, passed)]].set(jnp.asarray(sizes, jnp.int32))

    sizes = jnp.where(number % 4 == 0, named(heavy_load, number // 4), named(usual, number - number // 4 - 1))
    mixed = jax.random.permutation(jax.random.fold_in(own, 3), number_of)
    source_of, receiver = mixed[0:number_of // 2 * 2:2], mixed[1:number_of // 2 * 2:2]
    room = jnp.minimum(sizes[source_of] - 1, bound - sizes[receiver]) // 2
    room = jnp.where((source_of == sequence[0]) | (receiver == sequence[0]) | (sizes[receiver] == 0), 0, jnp.maximum(room, 0))
    passed = jax.random.randint(jax.random.fold_in(own, 4), (number_of // 2,), 0, 1 << 20) % (room + 1)
    sizes = sizes.at[source_of].add(-passed).at[receiver].add(passed)
    items = jnp.searchsorted(jnp.cumsum(sizes), jnp.arange(rows * top), side="right").astype(jnp.int32)
    grid = items.reshape(top, rows).T
    grid = grid[jax.random.permutation(jax.random.fold_in(own, 1), rows)]
    turn = jax.random.randint(jax.random.fold_in(own, 2), (rows, 1), 0, top)
    return jnp.take_along_axis(grid, (jnp.arange(top)[None, :] + turn) % top, axis=1)


def portions_of(number_of, total, limit, slope, full):
    loads = [(1 << 20) // math.isqrt(standing ** slope) + 1 for standing in range(1, number_of + 1)]
    largest = limit if full else min(limit, max(-(-total // number_of), total * loads[0] // sum(loads)))
    least = 1 if total - largest >= number_of - 1 else 0
    counts, rest = [largest] + [least] * (number_of - 1), total - largest - least * (number_of - 1)
    while rest > 0:
        candidates = [i for i in range(1, number_of) if counts[i] < largest] or [i for i in range(1, number_of) if counts[i] < limit]
        pool, remaining = sum([loads[i] for i in candidates]), rest
        for i in candidates:
            more = min(limit - counts[i], max(1, remaining * loads[i] // pool), rest)
            counts[i] = counts[i] + more
            rest = rest - more
    return np.array(counts)


def bell_draw(own_key, dims, width, limit, cuts=(), kind=jnp.bfloat16):
    values = width * jax.random.normal(own_key, dims, jnp.float32)
    if cuts:
        values = values * steps_of(own_key, dims, cuts, -0.22, 0.18)
    return jnp.clip(values, -limit, limit).astype(kind)


def setup_inputs(seed: int = 0) -> dict:
    streams_of = jax.random.split(jax.random.key(seed), 6)
    descriptors = bell_draw(streams_of[0], (ATOMS, D), 1.0, 6.0, ((0, 32),))
    expert_ids_keys = jax.random.split(jax.random.fold_in(streams_of[1], 1), ATOMS // ROWS_DEV)
    expert_ids_turns = jax.random.permutation(jax.random.fold_in(streams_of[1], 3), ATOMS // ROWS_DEV)
    expert_ids = jax.vmap(lambda own, number: deal_out(jax.random.fold_in(streams_of[1], 2), own, number, ROWS_DEV, EXPERTS, 1, CAP, 2))(expert_ids_keys, expert_ids_turns).reshape((ATOMS, 1))
    cotangent = bell_draw(streams_of[2], (ATOMS,), 1.0, 6.0, ((0, 32),))
    w1 = bell_draw(streams_of[3], (EXPERTS, D, H), D ** -0.5, 0.1875, ((0, 8),))
    w2 = bell_draw(streams_of[4], (EXPERTS, H), 0.1, 0.59765625, ((0, 8),))
    return dict(descriptors=descriptors, expert_ids=expert_ids, cotangent=cotangent, w1=w1, w2=w2)


def reference(descriptors, expert_ids, cotangent, w1, w2):
    device_count = N_EXPERT * N_REP
    slot_count = N_EXPERT * CAP
    route_ids = expert_ids.reshape(device_count, ROWS_DEV)
    member = (route_ids[:, :, None] == jnp.arange(N_EXPERT, dtype=jnp.int32)[None, None, :]).astype(jnp.int32)
    slot_rank = jnp.sum((jnp.cumsum(member, axis=1) - 1) * member, axis=2)
    slot_index = route_ids * CAP + slot_rank
    placement = (slot_index[:, :, None] == jnp.arange(slot_count, dtype=jnp.int32)[None, None, :]).astype(jnp.float32)
    packed_rows = jnp.einsum("drs,drk->dsk", placement, descriptors.reshape(device_count, ROWS_DEV, D).astype(jnp.float32)).astype(jnp.bfloat16)
    packed_cot = jnp.einsum("drs,dr->ds", placement, cotangent.reshape(device_count, ROWS_DEV).astype(jnp.float32))
    packed_rows = packed_rows.reshape(N_EXPERT, N_REP, N_EXPERT, CAP, D)
    packed_cot = packed_cot.reshape(N_EXPERT, N_REP, N_EXPERT, CAP)

    def one_expert(owner_index):
        slot_rows = lax.dynamic_index_in_dim(packed_rows, owner_index, 2, keepdims=False)
        slot_rows = jnp.transpose(slot_rows, (1, 0, 2, 3)).reshape(N_REP, slot_count, D).astype(jnp.float32)
        slot_cot = lax.dynamic_index_in_dim(packed_cot, owner_index, 2, keepdims=False)
        slot_cot = jnp.transpose(slot_cot, (1, 0, 2)).reshape(N_REP, slot_count)
        weight = lax.dynamic_index_in_dim(w1, owner_index, 0, keepdims=False).astype(jnp.float32)
        readout = lax.dynamic_index_in_dim(w2, owner_index, 0, keepdims=False).astype(jnp.float32)
        preact = jnp.einsum("rsk,kh->rsh", slot_rows, weight)
        gate_sig = jax.nn.sigmoid(preact)
        activated = preact * gate_sig
        energy = jnp.sum(activated * readout, axis=2).astype(jnp.bfloat16)
        hidden_grad = (slot_cot[:, :, None] * readout * gate_sig * (1.0 + preact * (1.0 - gate_sig))).astype(jnp.bfloat16)
        hidden_wide = hidden_grad.astype(jnp.float32)
        input_grad = jnp.einsum("rsh,kh->rsk", hidden_wide, weight).astype(jnp.bfloat16)
        partials = jnp.einsum("rsh,rsk->rhk", hidden_wide, slot_rows).astype(jnp.bfloat16)
        partials = lax.optimization_barrier(partials).astype(jnp.float32)
        weight_grad = jnp.sum(partials, axis=0).astype(jnp.bfloat16)
        readout_grad = jnp.sum(slot_cot[:, :, None] * activated, axis=(0, 1))
        return energy, input_grad, weight_grad, readout_grad

    energy, input_grad, w1_grad, w2_grad = lax.map(one_expert, jnp.arange(N_EXPERT, dtype=jnp.int32))
    energy = jnp.transpose(energy.reshape(N_EXPERT, N_REP, N_EXPERT, CAP), (2, 1, 0, 3)).reshape(device_count, slot_count)
    input_grad = jnp.transpose(input_grad.reshape(N_EXPERT, N_REP, N_EXPERT, CAP, D), (2, 1, 0, 3, 4)).reshape(device_count, slot_count, D)
    energies = jnp.einsum("drs,ds->dr", placement, energy.astype(jnp.float32)).reshape(ATOMS).astype(jnp.bfloat16)
    descriptor_grad = jnp.einsum("drs,dsk->drk", placement, input_grad.astype(jnp.float32)).reshape(ATOMS, D).astype(jnp.bfloat16)
    return energies, descriptor_grad, w1_grad, w2_grad
```

```python
import functools

import jax
import jax.numpy as jnp
from jax import lax
from jax.experimental import pallas as pl
from jax.experimental.pallas import tpu as pltpu
from jax.sharding import PartitionSpec as P

CAP = 12
LANES = 128
PLANE_ROWS = 512
F32, BF16 = jnp.float32, jnp.bfloat16
VMEM = pl.BlockSpec(memory_space=pltpu.VMEM)
SMEM = pl.BlockSpec(memory_space=pltpu.SMEM)


def call(kernel, out_shape, operands, scratch=(), flops=0, scalars=0):
    moved = sum(x.size * x.dtype.itemsize for x in jax.tree.leaves((out_shape, operands)))
    return pl.pallas_call(
        kernel,
        out_shape=out_shape,
        in_specs=[SMEM] * scalars + [VMEM] * (len(operands) - scalars),
        out_specs=jax.tree.map(lambda _: VMEM, out_shape),
        scratch_shapes=list(scratch),
        cost_estimate=pl.CostEstimate(flops=flops, bytes_accessed=moved, transcendentals=0),
        compiler_params=pltpu.CompilerParams(vmem_limit_bytes=48 << 20),
    )(*operands)


def swap(x, axis, k):
    return lax.ppermute(x, axis, [(i, i ^ k) for i in range(lax.axis_size(axis))])


def iota(shape, dim):
    return lax.broadcasted_iota(jnp.int32, shape, dim)


def dot(a, b, dims=((1,), (0,))):
    return lax.dot_general(a, b, (dims, ((), ())), preferred_element_type=F32)


def label_rows(rows_ref, ids_ref, cot_ref, out_ref):
    rows, width = rows_ref.shape
    eye = iota((rows, rows), 0) == iota((rows, rows), 1)

    def column(line):
        return jnp.sum(jnp.where(eye, jnp.broadcast_to(line, (rows, rows)), 0.0), axis=1, keepdims=True)

    lane = iota((rows, LANES), 1)
    cot = column(cot_ref[...].astype(F32))
    ids = column(ids_ref[...].astype(F32))
    out_ref[:, :width] = rows_ref[...]
    out_ref[:, width:] = jnp.where(lane == 0, cot, jnp.where(lane == 1, ids, 0.0)).astype(BF16)


def gate(preact):
    sig = 1.0 / (1.0 + jnp.exp(-preact))
    return sig, preact * sig


def own_plane(n, where_ref, *refs):
    blocks, (w1_ref, w2_ref), (even_ref, odd_ref, band_ref, readout_ref), (xs, hs) = (
        refs[:n], refs[n:n + 2], refs[n + 2:n + 6], refs[n + 6:])
    rows = blocks[0].shape[0]
    width, hidden = w1_ref.shape
    band = band_ref.shape[1]
    for k in range(n):
        xs[k * rows:(k + 1) * rows, :] = blocks[k][...]
    tags = xs[:, width:].astype(F32)
    mine = tags[:, 1:2] == where_ref[0].astype(F32)
    cot = jnp.where(mine, tags[:, 0:1], 0.0)
    energy = jnp.zeros((n * rows, 1), F32)
    for c in range(0, hidden, band):
        part = slice(c, c + band)
        preact = dot(xs[:, :width], w1_ref[:, part])
        sig, act = gate(preact)
        w2 = w2_ref[:, part].astype(F32)
        energy += jnp.sum(act * w2, axis=1, keepdims=True)
        hs[:, part] = (cot * w2 * sig * (1.0 + preact * (1.0 - sig))).astype(BF16)
        readout_ref[:, part] = jnp.sum(cot * act, axis=0, keepdims=True)
    band_ref[...] = hs[:, pl.ds(pl.multiple_of(where_ref[1] * band, band), band)]
    back = dot(hs[...], w1_ref[...], ((1,), (1,))).astype(BF16)
    tail = jnp.where((iota((n * rows, LANES), 1) == 0) & mine, energy, 0.0).astype(BF16)
    for k in range(n):
        out, at, here = (odd_ref if k % 2 else even_ref), slice(k // 2 * rows, (k // 2 + 1) * rows), slice(k * rows, (k + 1) * rows)
        out[at, :width] = back[here, :]
        out[at, width:] = tail[here, :]


def pick_slots(n, where_ref, *refs):
    blocks, outs, (xs,) = refs[:n], refs[n:-1], refs[-1:]
    rows, wide = blocks[0].shape
    total = n * rows
    width = wide - LANES
    for k in range(n):
        xs[k * rows:(k + 1) * rows, :] = blocks[k][...]
    ids = xs[:, width:].astype(F32)[:, 1:2].astype(jnp.int32)
    i, j = iota((total, total), 0), iota((total, total), 1)
    before = ((j < i) & (j // rows == i // rows)).astype(BF16)
    lane = iota((total, LANES), 1)
    member = ids == (where_ref[0] ^ (2 * lane))
    rank = dot(before, member.astype(BF16))
    slot = jnp.where(member, (iota((total, LANES), 0) // rows) * CAP + rank.astype(jnp.int32), -1)
    for d, out_ref in enumerate(outs):
        size = out_ref.shape[0]
        pick = (slot[:, d:d + 1] == iota((total, size), 1)).astype(BF16)
        out_ref[...] = dot(pick, xs[...], ((0,), (0,))).astype(BF16)


def add_blocks(even_ref, odd_ref, *outs):
    rows = outs[0].shape[0]
    for k, out_ref in enumerate(outs):
        at = slice(k * rows, (k + 1) * rows)
        out_ref[...] = even_ref[at, :] + odd_ref[at, :]


def add_returned(*refs):
    parts, (grad_ref, energy_ref) = refs[:-2], refs[-2:]
    rows, width = grad_ref.shape
    total = parts[0][...].astype(F32)
    for part in parts[1:]:
        total += part[...].astype(F32)
    grad_ref[...] = total[:, :width].astype(BF16)
    eye = iota((rows, rows), 0) == iota((rows, rows), 1)
    line = jnp.sum(jnp.where(eye, total[:, width:width + 1], 0.0), axis=0, keepdims=True)
    energy_ref[...] = line.astype(BF16)


def all_replicas(n, m, where_ref, *refs):
    slots, blocks = refs[:n], refs[n:n + m]
    w1_ref, w2_ref, band_ref, readout_ref, w1_grad_ref, w2_grad_ref, ys, xs = refs[n + m:]
    size, rows = slots[0].shape[0], blocks[0].shape[0]
    width, hidden = w1_ref.shape
    band = w1_grad_ref.shape[0]
    for k in range(n):
        ys[k * size:(k + 1) * size, :] = slots[k][...]
    for k in range(m):
        xs[k * rows:(k + 1) * rows, :] = blocks[k][:, :width]
    cot = ys[:, width:].astype(F32)[:, 0:1]
    bands = hidden // band
    for j in range(bands):
        at = where_ref[1] + j
        at = jnp.where(at >= bands, at - bands, at)
        part = pl.ds(pl.multiple_of(at * band, band), band)
        preact = dot(ys[:, :width], w1_ref[:, part])
        sig, act = gate(preact)
        w2_grad_ref[:, part] = readout_ref[:, part] + jnp.sum(cot * act, axis=0, keepdims=True)
        if j == 0:
            w2 = w2_ref[:, part].astype(F32)
            hidden_grad = (cot * w2 * sig * (1.0 + preact * (1.0 - sig))).astype(BF16)
            grad = dot(hidden_grad, ys[:, :width], ((0,), (0,)))
            grad += dot(band_ref[...], xs[...], ((0,), (0,)))
            w1_grad_ref[...] = grad.astype(BF16)


def by_blocks(descriptors, expert_ids, cotangent, w1, w2):
    owners, replicas = lax.axis_size("expert"), lax.axis_size("rep")
    rows, width = descriptors.shape
    wide = width + LANES
    weight, readout = w1[0], w2
    hidden = weight.shape[1]
    band = hidden // replicas
    where = jnp.stack([lax.axis_index("expert"), lax.axis_index("rep")]).astype(jnp.int32)
    shape = jax.ShapeDtypeStruct

    own = call(
        label_rows, shape((rows, wide), BF16),
        (descriptors, expert_ids.reshape(1, rows), cotangent.reshape(1, rows)),
    )
    far = [swap(own, "rep", k) for k in range(1, replicas)]
    even = [own] + [swap(own, "expert", k) for k in range(2, owners, 2)]
    odd = [swap(block, "expert", 1) for block in even]
    blocks = [block for pair in zip(even, odd) for block in pair]

    total = owners * rows
    even_back, odd_back, band_grad, readout_part = call(
        functools.partial(own_plane, owners),
        (
            shape((total // 2, wide), BF16), shape((total // 2, wide), BF16),
            shape((total, band), BF16), shape((1, hidden), F32),
        ),
        (where, *blocks, weight, readout),
        (pltpu.VMEM((total, wide), BF16), pltpu.VMEM((total, hidden), BF16)),
        flops=4 * total * width * hidden, scalars=1,
    )

    far += [swap(block, "expert", 1) for block in far]
    size = -(-len(far) * CAP // 16) * 16
    slots = call(
        functools.partial(pick_slots, len(far)),
        [shape((size, wide), BF16)] * (owners // 2),
        (where, *far),
        (pltpu.VMEM((len(far) * rows, wide), BF16),),
        flops=owners * size * len(far) * rows * wide, scalars=1,
    )
    slots = [slots[0]] + [swap(slots[k], "expert", 2 * k) for k in range(1, owners // 2)]

    odd_back = swap(odd_back, "expert", 1)
    back = call(add_blocks, [shape((rows, wide), BF16)] * (owners // 2), (even_back, odd_back))
    back = [back[0]] + [swap(back[k], "expert", 2 * k) for k in range(1, owners // 2)]

    w1_grad, w2_grad = call(
        functools.partial(all_replicas, len(slots), owners),
        (shape((band, width), BF16), shape((1, hidden), F32)),
        (where, *slots, *blocks, weight, readout, band_grad, readout_part),
        (pltpu.VMEM((len(slots) * size, wide), BF16), pltpu.VMEM((total, width), BF16)),
        flops=2 * len(slots) * size * width * (hidden + band) + 2 * total * width * band, scalars=1,
    )
    descriptor_grad, energies = call(
        add_returned, (shape((rows, width), BF16), shape((1, rows), BF16)), tuple(back)
    )
    return energies.reshape(rows), descriptor_grad, w1_grad[None], w2_grad


def by_slots(descriptors, expert_ids, cotangent, w1, w2):
    owners = lax.axis_size("expert")
    columns = descriptors.shape[1]
    slot_count = owners * CAP
    targets = expert_ids[:, 0]
    member = (targets[:, None] == jnp.arange(owners, dtype=jnp.int32)[None, :]).astype(jnp.int32)
    slot_rank = jnp.sum((jnp.cumsum(member, axis=0) - 1) * member, axis=1)
    placement = (
        (targets * CAP + slot_rank)[:, None] == jnp.arange(slot_count, dtype=jnp.int32)[None, :]
    ).astype(BF16)
    over_rows = ((0,), (0,))

    def exchange(slots):
        parted = slots.reshape(owners, CAP, *slots.shape[1:])
        moved = lax.all_to_all(parted, "expert", split_axis=0, concat_axis=0, tiled=True)
        return moved.reshape(slots.shape)

    slot_rows = exchange(dot(placement, descriptors, over_rows).astype(BF16))
    slot_cot = exchange(dot(placement, cotangent, over_rows).astype(BF16)).astype(F32)
    weight, readout = w1[0], w2[0].astype(F32)
    preact = dot(slot_rows, weight)
    sig = jax.nn.sigmoid(preact)
    activated = preact * sig
    energy = jnp.sum(activated * readout, axis=1).astype(BF16)
    hidden_grad = (slot_cot[:, None] * readout * sig * (1.0 + preact * (1.0 - sig))).astype(BF16)
    input_grad = dot(hidden_grad, weight, ((1,), (1,))).astype(BF16)
    energies = dot(placement, exchange(energy)).astype(BF16)
    descriptor_grad = dot(placement, exchange(input_grad)).astype(BF16)
    w2_grad = lax.psum(jnp.sum(slot_cot[:, None] * activated, axis=0), "rep")
    w1_grad = lax.psum_scatter(
        dot(hidden_grad, slot_rows, over_rows).astype(BF16), "rep", scatter_dimension=0, tiled=True
    )
    return energies, descriptor_grad, w1_grad[None], w2_grad[None]


def on_device(descriptors, *rest):
    few = descriptors.shape[0] * lax.axis_size("expert") <= PLANE_ROWS
    return (by_blocks if few else by_slots)(descriptors, *rest)


def solution(mesh):
    in_specs = (
        P(("expert", "rep"), None),
        P(("expert", "rep"), None),
        P(("expert", "rep")),
        P("expert", None, None),
        P("expert", None),
    )
    out_specs = (
        P(("expert", "rep")),
        P(("expert", "rep"), None),
        P("expert", "rep", None),
        P("expert", None),
    )
    return jax.shard_map(
        on_device, mesh=mesh, in_specs=in_specs, out_specs=out_specs, check_vma=False
    )
```

```python
import functools

import jax
import jax.numpy as jnp
from jax import lax
from jax.experimental import pallas as pl
from jax.experimental.pallas import tpu as pltpu
from jax.sharding import PartitionSpec as P

CAP = 12
LANES = 128
PLANE_ROWS = 512
WAIT = 5_000_000_000
F32, BF16 = jnp.float32, jnp.bfloat16
VMEM = pl.BlockSpec(memory_space=pltpu.VMEM)
SMEM = pl.BlockSpec(memory_space=pltpu.SMEM)
HBM = pl.BlockSpec(memory_space=pltpu.HBM)
DMA = pltpu.SemaphoreType.DMA


def call(kernel, out_shape, operands, scratch=(), flops=0, scalars=0, from_hbm=0, vmem=24):
    moved = sum(x.size * x.dtype.itemsize for x in jax.tree.leaves((out_shape, operands)))
    return pl.pallas_call(
        kernel,
        out_shape=out_shape,
        in_specs=[SMEM] * scalars + [VMEM] * (len(operands) - scalars - from_hbm) + [HBM] * from_hbm,
        out_specs=jax.tree.map(lambda _: VMEM, out_shape),
        scratch_shapes=list(scratch),
        cost_estimate=pl.CostEstimate(flops=flops, bytes_accessed=moved, transcendentals=0),
        compiler_params=pltpu.CompilerParams(vmem_limit_bytes=vmem << 20),
    )(*operands)


def swap(x, axis, k):
    return lax.ppermute(x, axis, [(i, i ^ k) for i in range(lax.axis_size(axis))])


def iota(shape, dim):
    return lax.broadcasted_iota(jnp.int32, shape, dim)


def dot(a, b, dims=((1,), (0,))):
    return lax.dot_general(a, b, (dims, ((), ())), preferred_element_type=F32)


def label_rows(rows_hbm, ids_hbm, cot_hbm, w2_hbm, out_ref, w2_ref, ids_ref, cot_ref, sems):
    rows, width = rows_hbm.shape
    copies = [
        pltpu.make_async_copy(ids_hbm, ids_ref, sems.at[0]),
        pltpu.make_async_copy(cot_hbm, cot_ref, sems.at[1]),
        pltpu.make_async_copy(rows_hbm, out_ref.at[:, :width], sems.at[2]),
        pltpu.make_async_copy(w2_hbm, w2_ref, sems.at[3]),
    ]
    for copy in copies:
        copy.start()
    eye = iota((rows, rows), 0) == iota((rows, rows), 1)

    def column(line):
        return jnp.sum(jnp.where(eye, jnp.broadcast_to(line, (rows, rows)), 0.0), axis=1, keepdims=True)

    lane = iota((rows, LANES), 1)
    copies[0].wait()
    copies[1].wait()
    cot = column(cot_ref[...].astype(F32))
    ids = column(ids_ref[...].astype(F32))
    out_ref[:, width:] = jnp.where(lane == 0, cot, jnp.where(lane == 1, ids, 0.0)).astype(BF16)
    copies[2].wait()
    copies[3].wait()


def stack_blocks(*refs):
    blocks, out_ref = refs[:-1], refs[-1]
    rows = blocks[0].shape[0]
    for k, block in enumerate(blocks):
        out_ref[k * rows:(k + 1) * rows, :] = block[...]


def gate(preact):
    sig = 1.0 / (1.0 + jnp.exp(-preact))
    return sig, preact * sig


def slots_of(ids, targets, rows, first):
    total = ids.shape[0]
    i, j = iota((total, total), 0), iota((total, total), 1)
    before = jnp.where((j < i) & ((i ^ j) < rows), 1.0, 0.0).astype(BF16)
    member = ids == targets
    rank = dot(before, jnp.where(member, 1.0, 0.0).astype(BF16))
    return jnp.where(member, first + rank.astype(jnp.int32), -1)


def block_of(total, rows):
    return iota((total, LANES), 0) >> rows.bit_length() - 1


def one_hot(slot, size):
    return jnp.where(slot == iota((slot.shape[0], size), 1), 1.0, 0.0).astype(BF16)


def tags_of(block, width):
    return block[:, width:].astype(F32)


def own_plane(chips, rows, where_ref, near_ref, other_ref, w1_ref, w2_ref, after_ref, *refs):
    outs, (band_ref, kept_ref, readout_ref, hs) = refs[:chips], refs[chips:]
    width, hidden = w1_ref.shape
    band = band_ref.shape[1]
    half = chips * rows
    kept = 2 * chips * CAP
    ids = jnp.concatenate([tags_of(ref, width)[:, 1:2] for ref in (near_ref, other_ref)], axis=0)
    block = block_of(2 * half, rows)
    first = jnp.where(block < chips, block * (2 * CAP), (block - chips) * (2 * CAP) + CAP)
    slot = slots_of(ids.astype(jnp.int32), where_ref[0], rows, first)[:, 0:1]
    picked = dot(one_hot(slot[:half], kept), near_ref[...], ((0,), (0,)))
    picked += dot(one_hot(slot[half:], kept), other_ref[...], ((0,), (0,)))
    kept_ref[...] = picked.astype(BF16)
    cot = tags_of(kept_ref, width)[:, 0:1]
    energy = jnp.zeros((kept, 1), F32)
    for c in range(0, hidden, band):
        part = slice(c, c + band)
        preact = dot(kept_ref[:, :width], w1_ref[:, part])
        sig, act = gate(preact)
        w2 = w2_ref[:, part].astype(F32)
        energy += jnp.sum(act * w2, axis=1, keepdims=True)
        hs[:, part] = (cot * w2 * sig * (1.0 + preact * (1.0 - sig))).astype(BF16)
        readout_ref[:, part] = jnp.sum(cot * act, axis=0, keepdims=True)
    band_ref[...] = hs[:, pl.ds(pl.multiple_of(where_ref[1] * band, band), band)]
    back = dot(hs[...], w1_ref[...], ((1,), (1,)))
    tail = jnp.where(iota((kept, LANES), 1) == 0, energy, 0.0)
    for k, out_ref in enumerate(outs):
        here = slice(2 * CAP * k, 2 * CAP * (k + 1))
        out_ref[:, :width] = back[here, :].astype(BF16)
        out_ref[:, width:] = tail[here, :].astype(BF16)


def pick_slots(rows, where_ref, far_ref, other_ref, *outs):
    half, wide = far_ref.shape
    size = outs[0].shape[0]
    ids = jnp.concatenate([tags_of(ref, wide - LANES)[:, 1:2] for ref in (far_ref, other_ref)], axis=0)
    targets = where_ref[0] ^ (2 * iota((2 * half, LANES), 1))
    slot = slots_of(ids.astype(jnp.int32), targets, rows, block_of(2 * half, rows) * CAP)
    for k, out_ref in enumerate(outs):
        pick = one_hot(slot[:, k:k + 1], size)
        rows_of_chip = dot(pick[:half], far_ref[...], ((0,), (0,)))
        rows_of_chip += dot(pick[half:], other_ref[...], ((0,), (0,)))
        out_ref[...] = rows_of_chip.astype(BF16)


def place_rows(n, where_ref, near_ref, other_ref, *refs):
    slots, (mine_ref, theirs_ref) = refs[:n], refs[-2:]
    rows, wide = mine_ref.shape
    ids = jnp.concatenate(
        [tags_of(ref.at[:rows, :], wide - LANES)[:, 1:2] for ref in (near_ref, other_ref)], axis=0
    )
    targets = where_ref[0] ^ (2 * iota((2 * rows, LANES), 1))
    slot = slots_of(ids.astype(jnp.int32), targets, rows, block_of(2 * rows, rows) * CAP)
    total = jnp.zeros((2 * rows, wide), F32)
    for k in range(n):
        total += dot(one_hot(slot[:, k:k + 1], 2 * CAP), slots[k][...])
    mine_ref[...] = total[:rows, :].astype(BF16)
    theirs_ref[...] = total[rows:, :].astype(BF16)


def add_cores(mine_ref, swapped_ref, grad_ref, energy_ref):
    rows, width = grad_ref.shape
    grad_ref[...] = mine_ref[:, :width] + swapped_ref[:, :width]
    column = (tags_of(mine_ref, width) + tags_of(swapped_ref, width))[:, 0:1]
    eye = iota((rows, rows), 0) == iota((rows, rows), 1)
    energy_ref[...] = jnp.sum(jnp.where(eye, column, 0.0), axis=0, keepdims=True).astype(BF16)


def all_replicas(n, where_ref, *refs):
    slots = refs[:n]
    kept_ref, w1_ref, w2_ref, band_ref, readout_ref, w1_grad_ref, w2_grad_ref, token_ref, ys, hs = refs[n:]
    size, kept = slots[0].shape[0], kept_ref.shape[0]
    width, hidden = w1_ref.shape
    band = w1_grad_ref.shape[0]
    new = n * size
    token_ref[...] = jnp.zeros(token_ref.shape, F32)
    for k in range(n):
        ys[k * size:(k + 1) * size, :] = slots[k][...]
    ys[new:, :] = kept_ref[...]
    hs[new:, :] = band_ref[...]
    cot = tags_of(ys, width)[:new, 0:1]
    bands = hidden // band
    for j in range(bands):
        at = where_ref[1] + j
        at = jnp.where(at >= bands, at - bands, at)
        part = pl.ds(pl.multiple_of(at * band, band), band)
        preact = dot(ys[:new, :width], w1_ref[:, part])
        sig, act = gate(preact)
        w2_grad_ref[:, part] = readout_ref[:, part] + jnp.sum(cot * act, axis=0, keepdims=True)
        if j == 0:
            w2 = w2_ref[:, part].astype(F32)
            hs[:new, :] = (cot * w2 * sig * (1.0 + preact * (1.0 - sig))).astype(BF16)
            w1_grad_ref[...] = dot(hs[...], ys[:, :width], ((0,), (0,))).astype(BF16)


def by_blocks(descriptors, expert_ids, cotangent, w1, w2):
    owners, replicas = lax.axis_size("expert"), lax.axis_size("rep")
    rows, width = descriptors.shape
    wide = width + LANES
    hidden = w1.shape[2]
    band = hidden // replicas
    chips = owners // 2
    kept = owners * CAP
    where = jnp.stack([lax.axis_index("expert"), lax.axis_index("rep")]).astype(jnp.int32)

    def shape(*dims, dtype=BF16):
        return jax.ShapeDtypeStruct(dims, dtype)

    def to_chips(blocks):
        return [blocks[0]] + [swap(blocks[k], "expert", 2 * k) for k in range(1, chips)]

    own, readout = call(
        label_rows, (shape(rows, wide), shape(1, hidden)),
        (descriptors, expert_ids.reshape(1, rows), cotangent.reshape(1, rows), w2),
        (pltpu.VMEM((1, rows), jnp.int32), pltpu.VMEM((1, rows), BF16), DMA((4,))),
        from_hbm=4, vmem=60,
    )
    weight = w1[0]
    far = [swap(own, "rep", k) for k in range(1, replicas)]
    near = to_chips([own] * chips)
    far = call(stack_blocks, shape(len(far) * rows, wide), tuple(far), flops=WAIT)
    near = call(stack_blocks, shape(chips * rows, wide), tuple(near), flops=WAIT)
    far_other = swap(far, "expert", 1)
    near_other = swap(near, "expert", 1)

    size = -(-2 * (replicas - 1) * CAP // 16) * 16
    chosen = call(
        functools.partial(pick_slots, rows), [shape(size, wide)] * chips, (where, far, far_other),
        flops=WAIT, scalars=1,
    )
    slots = to_chips(chosen)

    *back, band_grad, kept_rows, readout_part = call(
        functools.partial(own_plane, chips, rows),
        [shape(2 * CAP, wide)] * chips
        + [shape(kept, band), shape(kept, wide), shape(1, hidden, dtype=F32)],
        (where, near, near_other, weight, readout, chosen[0]),
        (pltpu.VMEM((kept, hidden), BF16),),
        flops=4 * kept * width * hidden, scalars=1,
    )
    back = to_chips(back)

    w1_grad, w2_grad, token = call(
        functools.partial(all_replicas, chips),
        (shape(band, width), shape(1, hidden, dtype=F32), shape(1, LANES, dtype=F32)),
        (where, *slots, kept_rows, weight, readout, band_grad, readout_part),
        (pltpu.VMEM((chips * size + kept, wide), BF16), pltpu.VMEM((chips * size + kept, band), BF16)),
        flops=2 * chips * size * width * (hidden + band), scalars=1,
    )

    mine, theirs = call(
        functools.partial(place_rows, chips), (shape(rows, wide), shape(rows, wide)),
        (where, near, near_other, *back, token), scalars=1,
    )
    descriptor_grad, energies = call(
        add_cores, (shape(rows, width), shape(1, rows)), (mine, swap(theirs, "expert", 1))
    )
    return energies.reshape(rows), descriptor_grad, w1_grad[None], w2_grad


def by_slots(descriptors, expert_ids, cotangent, w1, w2):
    owners = lax.axis_size("expert")
    columns = descriptors.shape[1]
    slot_count = owners * CAP
    targets = expert_ids[:, 0]
    member = (targets[:, None] == jnp.arange(owners, dtype=jnp.int32)[None, :]).astype(jnp.int32)
    slot_rank = jnp.sum((jnp.cumsum(member, axis=0) - 1) * member, axis=1)
    placement = (
        (targets * CAP + slot_rank)[:, None] == jnp.arange(slot_count, dtype=jnp.int32)[None, :]
    ).astype(BF16)
    over_rows = ((0,), (0,))

    def exchange(slots):
        parted = slots.reshape(owners, CAP, *slots.shape[1:])
        moved = lax.all_to_all(parted, "expert", split_axis=0, concat_axis=0, tiled=True)
        return moved.reshape(slots.shape)

    slot_rows = exchange(dot(placement, descriptors, over_rows).astype(BF16))
    slot_cot = exchange(dot(placement, cotangent, over_rows).astype(BF16)).astype(F32)
    weight, readout = w1[0], w2[0].astype(F32)
    preact = dot(slot_rows, weight)
    sig = jax.nn.sigmoid(preact)
    activated = preact * sig
    energy = jnp.sum(activated * readout, axis=1).astype(BF16)
    hidden_grad = (slot_cot[:, None] * readout * sig * (1.0 + preact * (1.0 - sig))).astype(BF16)
    input_grad = dot(hidden_grad, weight, ((1,), (1,))).astype(BF16)
    energies = dot(placement, exchange(energy)).astype(BF16)
    descriptor_grad = dot(placement, exchange(input_grad)).astype(BF16)
    w2_grad = lax.psum(jnp.sum(slot_cot[:, None] * activated, axis=0), "rep")
    w1_grad = lax.psum_scatter(
        dot(hidden_grad, slot_rows, over_rows).astype(BF16), "rep", scatter_dimension=0, tiled=True
    )
    return energies, descriptor_grad, w1_grad[None], w2_grad[None]


def on_device(descriptors, *rest):
    few = descriptors.shape[0] * lax.axis_size("expert") <= PLANE_ROWS
    return (by_blocks if few else by_slots)(descriptors, *rest)


def solution(mesh):
    in_specs = (
        P(("expert", "rep"), None),
        P(("expert", "rep"), None),
        P(("expert", "rep")),
        P("expert", None, None),
        P("expert", None),
    )
    out_specs = (
        P(("expert", "rep")),
        P(("expert", "rep"), None),
        P("expert", "rep", None),
        P("expert", None),
    )
    return jax.shard_map(
        on_device, mesh=mesh, in_specs=in_specs, out_specs=out_specs, check_vma=False
    )
```

```python
import functools

import jax
import jax.numpy as jnp
from jax import lax
from jax.experimental import pallas as pl
from jax.experimental.pallas import tpu as pltpu
from jax.sharding import PartitionSpec as P

CAP = 12
LANES = 128
PLANE_ROWS = 512
WAIT = 5_000_000_000
F32, BF16 = jnp.float32, jnp.bfloat16
VMEM = pl.BlockSpec(memory_space=pltpu.VMEM)
SMEM = pl.BlockSpec(memory_space=pltpu.SMEM)
HBM = pl.BlockSpec(memory_space=pltpu.HBM)
DMA = pltpu.SemaphoreType.DMA


def call(kernel, out_shape, operands, scratch=(), flops=0, scalars=0, from_hbm=0, vmem=24):
    moved = sum(x.size * x.dtype.itemsize for x in jax.tree.leaves((out_shape, operands)))
    return pl.pallas_call(
        kernel,
        out_shape=out_shape,
        in_specs=[SMEM] * scalars + [VMEM] * (len(operands) - scalars - from_hbm) + [HBM] * from_hbm,
        out_specs=jax.tree.map(lambda _: VMEM, out_shape),
        scratch_shapes=list(scratch),
        cost_estimate=pl.CostEstimate(flops=flops, bytes_accessed=moved, transcendentals=0),
        compiler_params=pltpu.CompilerParams(vmem_limit_bytes=vmem << 20),
    )(*operands)


def swap(x, axis, k):
    return lax.ppermute(x, axis, [(i, i ^ k) for i in range(lax.axis_size(axis))])


def iota(shape, dim):
    return lax.broadcasted_iota(jnp.int32, shape, dim)


def dot(a, b, dims=((1,), (0,))):
    return lax.dot_general(a, b, (dims, ((), ())), preferred_element_type=F32)


def label_rows(rows_hbm, ids_hbm, cot_hbm, w2_hbm, out_ref, w2_ref, ids_ref, cot_ref, sems):
    rows, width = rows_hbm.shape
    copies = [
        pltpu.make_async_copy(ids_hbm, ids_ref, sems.at[0]),
        pltpu.make_async_copy(cot_hbm, cot_ref, sems.at[1]),
        pltpu.make_async_copy(rows_hbm, out_ref.at[:, :width], sems.at[2]),
        pltpu.make_async_copy(w2_hbm, w2_ref, sems.at[3]),
    ]
    for copy in copies:
        copy.start()
    eye = iota((rows, rows), 0) == iota((rows, rows), 1)

    def column(line):
        return jnp.sum(jnp.where(eye, jnp.broadcast_to(line, (rows, rows)), 0.0), axis=1, keepdims=True)

    lane = iota((rows, LANES), 1)
    copies[0].wait()
    copies[1].wait()
    cot = column(cot_ref[...].astype(F32))
    ids = column(ids_ref[...].astype(F32))
    out_ref[:, width:] = jnp.where(lane == 0, cot, jnp.where(lane == 1, ids, 0.0)).astype(BF16)
    copies[2].wait()
    copies[3].wait()


def stack_blocks(*refs):
    blocks, out_ref = refs[:-1], refs[-1]
    rows = blocks[0].shape[0]
    for k, block in enumerate(blocks):
        out_ref[k * rows:(k + 1) * rows, :] = block[...]


def gate(preact):
    sig = 1.0 / (1.0 + jnp.exp(-preact))
    return sig, preact * sig


def slots_of(ids, targets, rows, first):
    total = ids.shape[0]
    i, j = iota((total, total), 0), iota((total, total), 1)
    before = jnp.where((j < i) & ((i ^ j) < rows), 1.0, 0.0).astype(BF16)
    member = ids == targets
    rank = dot(before, jnp.where(member, 1.0, 0.0).astype(BF16))
    return jnp.where(member, first + rank.astype(jnp.int32), -1)


def block_of(total, rows):
    return iota((total, LANES), 0) >> rows.bit_length() - 1


def one_hot(slot, size):
    return jnp.where(slot == iota((slot.shape[0], size), 1), 1.0, 0.0).astype(BF16)


def tags_of(block, width):
    return block[:, width:].astype(F32)


def own_plane(
    chips, rows, where_ref, near_ref, other_ref, w1_ref, w2_ref, after_ref,
    keep_ref, give_ref, band_ref, kept_ref, readout_ref, hs,
):
    width, hidden = w1_ref.shape
    band = band_ref.shape[1]
    half = chips * rows
    kept = 2 * chips * CAP
    ids = jnp.concatenate([tags_of(ref, width)[:, 1:2] for ref in (near_ref, other_ref)], axis=0)
    block = block_of(2 * half, rows)
    slot = slots_of(ids.astype(jnp.int32), where_ref[0], rows, block_of(2 * half, rows) * CAP)[:, 0:1]
    picked = dot(one_hot(slot[:half], kept), near_ref[...], ((0,), (0,)))
    picked += dot(one_hot(slot[half:], kept), other_ref[...], ((0,), (0,)))
    kept_ref[...] = picked.astype(BF16)
    cot = tags_of(kept_ref, width)[:, 0:1]
    energy = jnp.zeros((kept, 1), F32)
    for c in range(0, hidden, band):
        part = slice(c, c + band)
        preact = dot(kept_ref[:, :width], w1_ref[:, part])
        sig, act = gate(preact)
        w2 = w2_ref[:, part].astype(F32)
        energy += jnp.sum(act * w2, axis=1, keepdims=True)
        hs[:, part] = (cot * w2 * sig * (1.0 + preact * (1.0 - sig))).astype(BF16)
        readout_ref[:, part] = jnp.sum(cot * act, axis=0, keepdims=True)
    band_ref[...] = hs[:, pl.ds(pl.multiple_of(where_ref[1] * band, band), band)]
    back = dot(hs[...], w1_ref[...], ((1,), (1,)))
    tail = jnp.where(iota((kept, LANES), 1) == 0, energy, 0.0)
    for out_ref, part in ((keep_ref, slice(0, kept // 2)), (give_ref, slice(kept // 2, kept))):
        out_ref[:, :width] = back[part, :].astype(BF16)
        out_ref[:, width:] = tail[part, :].astype(BF16)


def join_cores(keep_ref, got_ref, *outs):
    keep, got = keep_ref[...].astype(F32), got_ref[...].astype(F32)
    for k, out_ref in enumerate(outs):
        part = slice(CAP * k, CAP * (k + 1))
        out_ref[...] = jnp.concatenate([keep[part, :], got[part, :]], axis=0).astype(BF16)


def pick_slots(rows, where_ref, far_ref, other_ref, *outs):
    half, wide = far_ref.shape
    size = outs[0].shape[0]
    ids = jnp.concatenate([tags_of(ref, wide - LANES)[:, 1:2] for ref in (far_ref, other_ref)], axis=0)
    targets = where_ref[0] ^ (2 * iota((2 * half, LANES), 1))
    slot = slots_of(ids.astype(jnp.int32), targets, rows, block_of(2 * half, rows) * CAP)
    for k, out_ref in enumerate(outs):
        pick = one_hot(slot[:, k:k + 1], size)
        rows_of_chip = dot(pick[:half], far_ref[...], ((0,), (0,)))
        rows_of_chip += dot(pick[half:], other_ref[...], ((0,), (0,)))
        out_ref[...] = rows_of_chip.astype(BF16)


def place_rows(n, where_ref, own_ref, *refs):
    slots, (grad_ref, energy_ref) = refs[:n], refs[-2:]
    rows, width = grad_ref.shape
    ids = tags_of(own_ref, width)[:, 1:2].astype(jnp.int32)
    lane = iota((rows, LANES), 1)
    slot = slots_of(ids, where_ref[0] ^ lane, rows, jnp.where(lane & 1 == 0, 0, CAP))
    total = jnp.zeros(own_ref.shape, F32)
    for k in range(n):
        pick = one_hot(slot[:, 2 * k:2 * k + 1], 2 * CAP) + one_hot(slot[:, 2 * k + 1:2 * k + 2], 2 * CAP)
        total += dot(pick, slots[k][...])
    grad_ref[...] = total[:, :width].astype(BF16)
    eye = iota((rows, rows), 0) == iota((rows, rows), 1)
    line = jnp.sum(jnp.where(eye, total[:, width:width + 1], 0.0), axis=0, keepdims=True)
    energy_ref[...] = line.astype(BF16)


def all_replicas(n, where_ref, *refs):
    slots = refs[:n]
    kept_ref, w1_ref, w2_ref, band_ref, readout_ref, w1_grad_ref, w2_grad_ref, token_ref, ys, hs = refs[n:]
    size, kept = slots[0].shape[0], kept_ref.shape[0]
    width, hidden = w1_ref.shape
    band = w1_grad_ref.shape[0]
    new = n * size
    token_ref[...] = jnp.zeros(token_ref.shape, F32)
    for k in range(n):
        ys[k * size:(k + 1) * size, :] = slots[k][...]
    ys[new:, :] = kept_ref[...]
    hs[new:, :] = band_ref[...]
    cot = tags_of(ys, width)[:new, 0:1]
    bands = hidden // band
    for j in range(bands):
        at = where_ref[1] + j
        at = jnp.where(at >= bands, at - bands, at)
        part = pl.ds(pl.multiple_of(at * band, band), band)
        preact = dot(ys[:new, :width], w1_ref[:, part])
        sig, act = gate(preact)
        w2_grad_ref[:, part] = readout_ref[:, part] + jnp.sum(cot * act, axis=0, keepdims=True)
        if j == 0:
            w2 = w2_ref[:, part].astype(F32)
            hs[:new, :] = (cot * w2 * sig * (1.0 + preact * (1.0 - sig))).astype(BF16)
            w1_grad_ref[...] = dot(hs[...], ys[:, :width], ((0,), (0,))).astype(BF16)


def by_blocks(descriptors, expert_ids, cotangent, w1, w2):
    owners, replicas = lax.axis_size("expert"), lax.axis_size("rep")
    rows, width = descriptors.shape
    wide = width + LANES
    hidden = w1.shape[2]
    band = hidden // replicas
    chips = owners // 2
    kept = owners * CAP
    where = jnp.stack([lax.axis_index("expert"), lax.axis_index("rep")]).astype(jnp.int32)

    def shape(*dims, dtype=BF16):
        return jax.ShapeDtypeStruct(dims, dtype)

    def to_chips(blocks):
        return [blocks[0]] + [swap(blocks[k], "expert", 2 * k) for k in range(1, chips)]

    own, readout = call(
        label_rows, (shape(rows, wide), shape(1, hidden)),
        (descriptors, expert_ids.reshape(1, rows), cotangent.reshape(1, rows), w2),
        (pltpu.VMEM((1, rows), jnp.int32), pltpu.VMEM((1, rows), BF16), DMA((4,))),
        from_hbm=4, vmem=60,
    )
    weight = w1[0]
    far = [swap(own, "rep", k) for k in range(1, replicas)]
    far = call(stack_blocks, shape(len(far) * rows, wide), tuple(far), flops=WAIT)
    far_other = swap(far, "expert", 1)
    near = to_chips([own] * chips)
    near = call(stack_blocks, shape(chips * rows, wide), tuple(near), flops=WAIT)
    near_other = swap(near, "expert", 1)

    size = 2 * (replicas - 1) * CAP
    chosen = call(
        functools.partial(pick_slots, rows), [shape(size, wide)] * chips, (where, far, far_other),
        flops=WAIT, scalars=1,
    )
    slots = to_chips(chosen)

    keep, give, band_grad, kept_rows, readout_part = call(
        functools.partial(own_plane, chips, rows),
        [shape(kept // 2, wide), shape(kept // 2, wide), shape(kept, band), shape(kept, wide), shape(1, hidden, dtype=F32)],
        (where, near, near_other, weight, readout, chosen[0]),
        (pltpu.VMEM((kept, hidden), BF16),),
        flops=4 * kept * width * hidden, scalars=1,
    )
    got = swap(give, "expert", 1)
    back = to_chips(call(join_cores, [shape(2 * CAP, wide)] * chips, (keep, got)))

    w1_grad, w2_grad, token = call(
        functools.partial(all_replicas, chips),
        (shape(band, width), shape(1, hidden, dtype=F32), shape(1, LANES, dtype=F32)),
        (where, *slots, kept_rows, weight, readout, band_grad, readout_part),
        (pltpu.VMEM((chips * size + kept, wide), BF16), pltpu.VMEM((chips * size + kept, band), BF16)),
        flops=4 * WAIT, scalars=1,
    )

    descriptor_grad, energies = call(
        functools.partial(place_rows, chips), (shape(rows, width), shape(1, rows)),
        (where, own, *back, token), scalars=1,
    )
    return energies.reshape(rows), descriptor_grad, w1_grad[None], w2_grad


def by_slots(descriptors, expert_ids, cotangent, w1, w2):
    owners = lax.axis_size("expert")
    columns = descriptors.shape[1]
    slot_count = owners * CAP
    targets = expert_ids[:, 0]
    member = (targets[:, None] == jnp.arange(owners, dtype=jnp.int32)[None, :]).astype(jnp.int32)
    slot_rank = jnp.sum((jnp.cumsum(member, axis=0) - 1) * member, axis=1)
    placement = (
        (targets * CAP + slot_rank)[:, None] == jnp.arange(slot_count, dtype=jnp.int32)[None, :]
    ).astype(BF16)
    over_rows = ((0,), (0,))

    def exchange(slots):
        parted = slots.reshape(owners, CAP, *slots.shape[1:])
        moved = lax.all_to_all(parted, "expert", split_axis=0, concat_axis=0, tiled=True)
        return moved.reshape(slots.shape)

    slot_rows = exchange(dot(placement, descriptors, over_rows).astype(BF16))
    slot_cot = exchange(dot(placement, cotangent, over_rows).astype(BF16)).astype(F32)
    weight, readout = w1[0], w2[0].astype(F32)
    preact = dot(slot_rows, weight)
    sig = jax.nn.sigmoid(preact)
    activated = preact * sig
    energy = jnp.sum(activated * readout, axis=1).astype(BF16)
    hidden_grad = (slot_cot[:, None] * readout * sig * (1.0 + preact * (1.0 - sig))).astype(BF16)
    input_grad = dot(hidden_grad, weight, ((1,), (1,))).astype(BF16)
    energies = dot(placement, exchange(energy)).astype(BF16)
    descriptor_grad = dot(placement, exchange(input_grad)).astype(BF16)
    w2_grad = lax.psum(jnp.sum(slot_cot[:, None] * activated, axis=0), "rep")
    w1_grad = lax.psum_scatter(
        dot(hidden_grad, slot_rows, over_rows).astype(BF16), "rep", scatter_dimension=0, tiled=True
    )
    return energies, descriptor_grad, w1_grad[None], w2_grad[None]


def on_device(descriptors, *rest):
    few = descriptors.shape[0] * lax.axis_size("expert") <= PLANE_ROWS
    return (by_blocks if few else by_slots)(descriptors, *rest)


def solution(mesh):
    in_specs = (
        P(("expert", "rep"), None),
        P(("expert", "rep"), None),
        P(("expert", "rep")),
        P("expert", None, None),
        P("expert", None),
    )
    out_specs = (
        P(("expert", "rep")),
        P(("expert", "rep"), None),
        P("expert", "rep", None),
        P("expert", None),
    )
    return jax.shard_map(
        on_device, mesh=mesh, in_specs=in_specs, out_specs=out_specs, check_vma=False
    )
```

```python
import functools

import jax
import jax.numpy as jnp
from jax import lax
from jax.experimental import pallas as pl
from jax.experimental.pallas import tpu as pltpu
from jax.sharding import PartitionSpec as P

CAP = 12
LANES = 128
PLANE_ROWS = 512
WAIT = 5_000_000_000
F32, BF16 = jnp.float32, jnp.bfloat16
VMEM = pl.BlockSpec(memory_space=pltpu.VMEM)
SMEM = pl.BlockSpec(memory_space=pltpu.SMEM)
HBM = pl.BlockSpec(memory_space=pltpu.HBM)
DMA = pltpu.SemaphoreType.DMA


def call(kernel, out_shape, operands, scratch=(), flops=0, scalars=0, hbm_outs=0):
    outs = jax.tree.leaves(out_shape)
    specs = [HBM] * hbm_outs + [VMEM] * (len(outs) - hbm_outs)
    moved = sum(x.size * x.dtype.itemsize for x in jax.tree.leaves((out_shape, operands)))
    return pl.pallas_call(
        kernel,
        out_shape=out_shape,
        in_specs=[SMEM] * scalars + [VMEM] * (len(operands) - scalars),
        out_specs=jax.tree.unflatten(jax.tree.structure(out_shape), specs),
        scratch_shapes=list(scratch),
        cost_estimate=pl.CostEstimate(flops=flops, bytes_accessed=moved, transcendentals=0),
        compiler_params=pltpu.CompilerParams(vmem_limit_bytes=24 << 20),
    )(*operands)


def swap(x, axis, k):
    return lax.ppermute(x, axis, [(i, i ^ k) for i in range(lax.axis_size(axis))])


def iota(shape, dim):
    return lax.broadcasted_iota(jnp.int32, shape, dim)


def dot(a, b, dims=((1,), (0,))):
    return lax.dot_general(a, b, (dims, ((), ())), preferred_element_type=F32)


def begin(where_ref, token_ref):
    token_ref[...] = jnp.zeros(token_ref.shape, F32)


def label_rows(rows_ref, ids_ref, cot_ref, after_ref, out_ref):
    rows, width = rows_ref.shape
    i, j = iota((rows, rows), 0), iota((rows, rows), 1)

    def column(square):
        return jnp.sum(square, axis=1, keepdims=True)

    ids_line = jnp.broadcast_to(ids_ref[...].astype(F32), (rows, rows))
    cot_line = jnp.broadcast_to(cot_ref[...].astype(F32), (rows, rows))
    ids = column(jnp.where(i == j, ids_line, 0.0))
    cot = column(jnp.where(i == j, cot_line, 0.0))
    rank = column(jnp.where((j < i) & (ids_line == ids), 1.0, 0.0))
    lane = iota((rows, LANES), 1)
    tags = jnp.where(lane == 0, cot, jnp.where(lane == 1, ids, jnp.where(lane == 2, rank, 0.0)))
    out_ref[:, :width] = rows_ref[...]
    out_ref[:, width:] = tags.astype(BF16)


def stack_blocks(*refs):
    blocks, out_ref = refs[:-1], refs[-1]
    rows = blocks[0].shape[0]
    for k, block in enumerate(blocks):
        out_ref[k * rows:(k + 1) * rows, :] = block[...]


def gate(preact):
    sig = 1.0 / (1.0 + jnp.exp(-preact))
    return sig, preact * sig


def ids_and_ranks(*refs):
    tags = [ref[:, ref.shape[1] - LANES:].astype(F32)[:, 1:3] for ref in refs]
    tags = (tags[0] if len(tags) == 1 else jnp.concatenate(tags, axis=0)).astype(jnp.int32)
    return tags[:, 0:1], tags[:, 1:2]


def first_slot(total, rows):
    return (iota((total, 1), 0) >> rows.bit_length() - 1) * CAP


def one_hot(slot, size):
    return jnp.where(slot == iota((slot.shape[0], size), 1), 1.0, 0.0).astype(BF16)


def own_plane(
    chips, rows, where_ref, near_ref, other_ref, w1_ref, w2_ref, after_ref,
    keep_ref, give_ref, band_ref, kept_ref, readout_ref, hs,
):
    width, hidden = w1_ref.shape
    band = band_ref.shape[1]
    half = chips * rows
    kept = 2 * chips * CAP
    ids, ranks = ids_and_ranks(near_ref, other_ref)
    slot = jnp.where(ids == where_ref[0], first_slot(2 * half, rows) + ranks, -1)
    picked = dot(one_hot(slot[:half], kept), near_ref[...], ((0,), (0,)))
    picked += dot(one_hot(slot[half:], kept), other_ref[...], ((0,), (0,)))
    kept_ref[...] = picked.astype(BF16)
    cot = kept_ref[:, width:].astype(F32)[:, 0:1]
    energy = jnp.zeros((kept, 1), F32)
    for c in range(0, hidden, band):
        part = slice(c, c + band)
        preact = dot(kept_ref[:, :width], w1_ref[:, part])
        sig, act = gate(preact)
        w2 = w2_ref[:, part].astype(F32)
        energy += jnp.sum(act * w2, axis=1, keepdims=True)
        hs[:, part] = (cot * w2 * sig * (1.0 + preact * (1.0 - sig))).astype(BF16)
        readout_ref[:, part] = jnp.sum(cot * act, axis=0, keepdims=True)
    band_ref[...] = hs[:, pl.ds(pl.multiple_of(where_ref[1] * band, band), band)]
    back = dot(hs[...], w1_ref[...], ((1,), (1,)))
    tail = jnp.where(iota((kept, LANES), 1) == 0, energy, 0.0)
    for out_ref, part in ((keep_ref, slice(0, kept // 2)), (give_ref, slice(kept // 2, kept))):
        out_ref[:, :width] = back[part, :].astype(BF16)
        out_ref[:, width:] = tail[part, :].astype(BF16)


def join_cores(keep_ref, got_ref, *outs):
    keep, got = keep_ref[...].astype(F32), got_ref[...].astype(F32)
    for k, out_ref in enumerate(outs):
        part = slice(CAP * k, CAP * (k + 1))
        out_ref[...] = jnp.concatenate([keep[part, :], got[part, :]], axis=0).astype(BF16)


def pick_slots(rows, where_ref, far_ref, other_ref, *outs):
    half = far_ref.shape[0]
    size = outs[0].shape[0]
    ids, ranks = ids_and_ranks(far_ref, other_ref)
    apart = ids ^ where_ref[0]
    slot = jnp.where(apart & 1 == 0, (apart >> 1) * size + first_slot(2 * half, rows) + ranks, -1)
    pick = one_hot(slot, len(outs) * size)
    picked = dot(pick[:half], far_ref[...], ((0,), (0,)))
    picked += dot(pick[half:], other_ref[...], ((0,), (0,)))
    for k, out_ref in enumerate(outs):
        out_ref[...] = picked[k * size:(k + 1) * size, :].astype(BF16)


def place_rows(n, where_ref, own_ref, *refs):
    slots, (grad_ref, energy_ref) = refs[:n], refs[-2:]
    rows, width = grad_ref.shape
    size = slots[0].shape[0]
    ids, ranks = ids_and_ranks(own_ref)
    apart = ids ^ where_ref[0]
    slot = (apart >> 1) * size + (apart & 1) * CAP + ranks
    total = dot(one_hot(slot, size), slots[0][...])
    for k in range(1, n):
        total += dot(one_hot(slot - k * size, size), slots[k][...])
    grad_ref[...] = total[:, :width].astype(BF16)
    eye = iota((rows, rows), 0) == iota((rows, rows), 1)
    line = jnp.sum(jnp.where(eye, total[:, width:width + 1], 0.0), axis=0, keepdims=True)
    energy_ref[...] = line.astype(BF16)


def all_replicas(n, where_ref, *refs):
    slots = refs[:n]
    kept_ref, w1_ref, w2_ref, band_ref, readout_ref, w1_grad_hbm, w2_grad_ref, token_ref = refs[n:n + 8]
    ys, hs, w1_grad_ref, sem = refs[n + 8:]
    size, kept = slots[0].shape[0], kept_ref.shape[0]
    width, hidden = w1_ref.shape
    band = band_ref.shape[1]
    new = n * size
    token_ref[...] = jnp.zeros(token_ref.shape, F32)
    for k in range(n):
        ys[k * size:(k + 1) * size, :] = slots[k][...]
    ys[new:, :] = kept_ref[...]
    hs[new:, :] = band_ref[...]
    cot = ys[:new, width:].astype(F32)[:, 0:1]
    bands = hidden // band
    for j in range(bands):
        at = where_ref[1] + j
        at = jnp.where(at >= bands, at - bands, at)
        part = pl.ds(pl.multiple_of(at * band, band), band)
        preact = dot(ys[:new, :width], w1_ref[:, part])
        sig, act = gate(preact)
        w2_grad_ref[:, part] = readout_ref[:, part] + jnp.sum(cot * act, axis=0, keepdims=True)
        if j == 0:
            w2 = w2_ref[:, part].astype(F32)
            hs[:new, :] = (cot * w2 * sig * (1.0 + preact * (1.0 - sig))).astype(BF16)
            w1_grad_ref[...] = dot(hs[...], ys[:, :width], ((0,), (0,))).astype(BF16)
            copy = pltpu.make_async_copy(w1_grad_ref, w1_grad_hbm, sem)
            copy.start()
    copy.wait()


def by_blocks(descriptors, expert_ids, cotangent, w1, w2):
    owners, replicas = lax.axis_size("expert"), lax.axis_size("rep")
    rows, width = descriptors.shape
    wide = width + LANES
    hidden = w1.shape[2]
    band = hidden // replicas
    chips = owners // 2
    kept = owners * CAP
    where = jnp.stack([lax.axis_index("expert"), lax.axis_index("rep")]).astype(jnp.int32)

    def shape(*dims, dtype=BF16):
        return jax.ShapeDtypeStruct(dims, dtype)

    def to_chips(blocks):
        return [blocks[0]] + [swap(blocks[k], "expert", 2 * k) for k in range(1, chips)]

    begun = call(begin, shape(1, LANES, dtype=F32), (where,), flops=WAIT, scalars=1)
    own = call(
        label_rows, shape(rows, wide),
        (descriptors, expert_ids.reshape(1, rows), cotangent.reshape(1, rows), begun),
    )
    readout = w2
    weight = w1[0]
    far = [swap(own, "rep", k) for k in range(1, replicas)]
    far = call(stack_blocks, shape(len(far) * rows, wide), tuple(far), flops=WAIT)
    far_other = swap(far, "expert", 1)
    near = to_chips([own] * chips)
    near = call(stack_blocks, shape(chips * rows, wide), tuple(near), flops=WAIT)
    near_other = swap(near, "expert", 1)

    size = 2 * (replicas - 1) * CAP
    chosen = call(
        functools.partial(pick_slots, rows), [shape(size, wide)] * chips, (where, far, far_other),
        flops=WAIT, scalars=1,
    )
    slots = to_chips(chosen)

    keep, give, band_grad, kept_rows, readout_part = call(
        functools.partial(own_plane, chips, rows),
        [shape(kept // 2, wide), shape(kept // 2, wide), shape(kept, band), shape(kept, wide), shape(1, hidden, dtype=F32)],
        (where, near, near_other, weight, readout, chosen[0]),
        (pltpu.VMEM((kept, hidden), BF16),),
        flops=4 * kept * width * hidden, scalars=1,
    )
    got = swap(give, "expert", 1)
    back = to_chips(call(join_cores, [shape(2 * CAP, wide)] * chips, (keep, got)))

    w1_grad, w2_grad, token = call(
        functools.partial(all_replicas, chips),
        (shape(band, width), shape(1, hidden, dtype=F32), shape(1, LANES, dtype=F32)),
        (where, *slots, kept_rows, weight, readout, band_grad, readout_part),
        (
            pltpu.VMEM((chips * size + kept, wide), BF16), pltpu.VMEM((chips * size + kept, band), BF16),
            pltpu.VMEM((band, width), BF16), DMA,
        ),
        flops=4 * WAIT, scalars=1, hbm_outs=1,
    )

    descriptor_grad, energies = call(
        functools.partial(place_rows, chips), (shape(rows, width), shape(1, rows)),
        (where, own, *back, token), scalars=1,
    )
    return energies.reshape(rows), descriptor_grad, w1_grad[None], w2_grad


def by_slots(descriptors, expert_ids, cotangent, w1, w2):
    owners = lax.axis_size("expert")
    columns = descriptors.shape[1]
    slot_count = owners * CAP
    targets = expert_ids[:, 0]
    member = (targets[:, None] == jnp.arange(owners, dtype=jnp.int32)[None, :]).astype(jnp.int32)
    slot_rank = jnp.sum((jnp.cumsum(member, axis=0) - 1) * member, axis=1)
    placement = (
        (targets * CAP + slot_rank)[:, None] == jnp.arange(slot_count, dtype=jnp.int32)[None, :]
    ).astype(BF16)
    over_rows = ((0,), (0,))

    def exchange(slots):
        parted = slots.reshape(owners, CAP, *slots.shape[1:])
        moved = lax.all_to_all(parted, "expert", split_axis=0, concat_axis=0, tiled=True)
        return moved.reshape(slots.shape)

    slot_rows = exchange(dot(placement, descriptors, over_rows).astype(BF16))
    slot_cot = exchange(dot(placement, cotangent, over_rows).astype(BF16)).astype(F32)
    weight, readout = w1[0], w2[0].astype(F32)
    preact = dot(slot_rows, weight)
    sig = jax.nn.sigmoid(preact)
    activated = preact * sig
    energy = jnp.sum(activated * readout, axis=1).astype(BF16)
    hidden_grad = (slot_cot[:, None] * readout * sig * (1.0 + preact * (1.0 - sig))).astype(BF16)
    input_grad = dot(hidden_grad, weight, ((1,), (1,))).astype(BF16)
    energies = dot(placement, exchange(energy)).astype(BF16)
    descriptor_grad = dot(placement, exchange(input_grad)).astype(BF16)
    w2_grad = lax.psum(jnp.sum(slot_cot[:, None] * activated, axis=0), "rep")
    w1_grad = lax.psum_scatter(
        dot(hidden_grad, slot_rows, over_rows).astype(BF16), "rep", scatter_dimension=0, tiled=True
    )
    return energies, descriptor_grad, w1_grad[None], w2_grad[None]


def on_device(descriptors, *rest):
    few = descriptors.shape[0] * lax.axis_size("expert") <= PLANE_ROWS
    return (by_blocks if few else by_slots)(descriptors, *rest)


def solution(mesh):
    in_specs = (
        P(("expert", "rep"), None),
        P(("expert", "rep"), None),
        P(("expert", "rep")),
        P("expert", None, None),
        P("expert", None),
    )
    out_specs = (
        P(("expert", "rep")),
        P(("expert", "rep"), None),
        P("expert", "rep", None),
        P("expert", None),
    )
    return jax.shard_map(
        on_device, mesh=mesh, in_specs=in_specs, out_specs=out_specs, check_vma=False
    )
```

```python
import functools

import jax
import jax.numpy as jnp
from jax import lax
from jax.experimental import pallas as pl
from jax.experimental.pallas import tpu as pltpu
from jax.sharding import PartitionSpec as P

CAP = 12
LANES = 128
PLANE_ROWS = 512
WAIT = 5_000_000_000
F32, BF16 = jnp.float32, jnp.bfloat16
VMEM = pl.BlockSpec(memory_space=pltpu.VMEM)
SMEM = pl.BlockSpec(memory_space=pltpu.SMEM)
HBM = pl.BlockSpec(memory_space=pltpu.HBM)
DMA = pltpu.SemaphoreType.DMA


def call(kernel, out_shape, operands, scratch=(), flops=0, scalars=0, hbm_outs=0):
    outs = jax.tree.leaves(out_shape)
    specs = [HBM] * hbm_outs + [VMEM] * (len(outs) - hbm_outs)
    moved = sum(x.size * x.dtype.itemsize for x in jax.tree.leaves((out_shape, operands)))
    return pl.pallas_call(
        kernel,
        out_shape=out_shape,
        in_specs=[SMEM] * scalars + [VMEM] * (len(operands) - scalars),
        out_specs=jax.tree.unflatten(jax.tree.structure(out_shape), specs),
        scratch_shapes=list(scratch),
        cost_estimate=pl.CostEstimate(flops=flops, bytes_accessed=moved, transcendentals=0),
        compiler_params=pltpu.CompilerParams(vmem_limit_bytes=24 << 20),
    )(*operands)


def swap(x, axis, k):
    return lax.ppermute(x, axis, [(i, i ^ k) for i in range(lax.axis_size(axis))])


def iota(shape, dim):
    return lax.broadcasted_iota(jnp.int32, shape, dim)


def dot(a, b, dims=((1,), (0,))):
    return lax.dot_general(a, b, (dims, ((), ())), preferred_element_type=F32)


def begin(where_ref, token_ref):
    token_ref[...] = jnp.zeros(token_ref.shape, F32)


def label_rows(rows_ref, ids_ref, cot_ref, after_ref, out_ref):
    rows, width = rows_ref.shape
    i, j = iota((rows, rows), 0), iota((rows, rows), 1)

    def column(square):
        return jnp.sum(square, axis=1, keepdims=True)

    ids_line = jnp.broadcast_to(ids_ref[...].astype(F32), (rows, rows))
    cot_line = jnp.broadcast_to(cot_ref[...].astype(F32), (rows, rows))
    ids = column(jnp.where(i == j, ids_line, 0.0))
    cot = column(jnp.where(i == j, cot_line, 0.0))
    rank = column(jnp.where((j < i) & (ids_line == ids), 1.0, 0.0))
    lane = iota((rows, LANES), 1)
    tags = jnp.where(lane == 0, cot, jnp.where(lane == 1, ids, jnp.where(lane == 2, rank, 0.0)))
    out_ref[:, :width] = rows_ref[...]
    out_ref[:, width:] = tags.astype(BF16)


def stack_blocks(*refs):
    blocks, out_ref = refs[:-1], refs[-1]
    rows = blocks[0].shape[0]
    for k, block in enumerate(blocks):
        out_ref[k * rows:(k + 1) * rows, :] = block[...]


def gate(preact):
    sig = 0.5 * jnp.tanh(0.5 * preact) + 0.5
    return sig, preact * sig


def ids_and_ranks(*refs):
    tags = [ref[:, ref.shape[1] - LANES:].astype(F32)[:, 1:3] for ref in refs]
    tags = (tags[0] if len(tags) == 1 else jnp.concatenate(tags, axis=0)).astype(jnp.int32)
    return tags[:, 0:1], tags[:, 1:2]


def first_slot(total, rows):
    return (iota((total, 1), 0) >> rows.bit_length() - 1) * CAP


def one_hot(slot, size):
    return jnp.where(slot == iota((slot.shape[0], size), 1), 1.0, 0.0).astype(BF16)


def own_plane(
    chips, rows, where_ref, near_ref, other_ref, w1_ref, w2_ref, after_ref,
    keep_ref, give_ref, band_ref, kept_ref, readout_ref, spread_ref, xs, hs,
):
    width, hidden = w1_ref.shape
    band = band_ref.shape[1]
    half = chips * rows
    kept = 2 * chips * CAP
    ids, ranks = ids_and_ranks(near_ref, other_ref)
    slot = jnp.where(ids == where_ref[0], first_slot(2 * half, rows) + ranks, -1)
    apart = ids[:rows] ^ where_ref[0]
    spread_ref[...] = one_hot((apart >> 1) * (2 * CAP) + (apart & 1) * CAP + ranks[:rows], kept)
    xs[:half, :] = near_ref[...]
    xs[half:, :] = other_ref[...]
    kept_ref[...] = dot(one_hot(slot, kept), xs[...], ((0,), (0,))).astype(BF16)
    cot = kept_ref[:, width:].astype(F32)[:, 0:1]
    energy = jnp.zeros((kept, 1), F32)
    for c in range(0, hidden, band):
        part = slice(c, c + band)
        preact = dot(kept_ref[:, :width], w1_ref[:, part])
        sig, act = gate(preact)
        w2 = w2_ref[:, part].astype(F32)
        energy += jnp.sum(act * w2, axis=1, keepdims=True)
        hs[:, part] = (cot * w2 * sig * (1.0 + preact * (1.0 - sig))).astype(BF16)
        readout_ref[:, part] = jnp.sum(cot * act, axis=0, keepdims=True)
    band_ref[...] = hs[:, pl.ds(pl.multiple_of(where_ref[1] * band, band), band)]
    back = dot(hs[...], w1_ref[...], ((1,), (1,)))
    tail = jnp.where(iota((kept, LANES), 1) == 0, energy, 0.0)
    for out_ref, part in ((keep_ref, slice(0, kept // 2)), (give_ref, slice(kept // 2, kept))):
        out_ref[:, :width] = back[part, :].astype(BF16)
        out_ref[:, width:] = tail[part, :].astype(BF16)


def join_cores(keep_ref, got_ref, *outs):
    keep, got = keep_ref[...].astype(F32), got_ref[...].astype(F32)
    for k, out_ref in enumerate(outs):
        part = slice(CAP * k, CAP * (k + 1))
        out_ref[...] = jnp.concatenate([keep[part, :], got[part, :]], axis=0).astype(BF16)


def pick_slots(rows, where_ref, far_ref, other_ref, *refs):
    outs, xs = refs[:-1], refs[-1]
    half = far_ref.shape[0]
    size = outs[0].shape[0]
    ids, ranks = ids_and_ranks(far_ref, other_ref)
    apart = ids ^ where_ref[0]
    slot = jnp.where(apart & 1 == 0, (apart >> 1) * size + first_slot(2 * half, rows) + ranks, -1)
    xs[:half, :] = far_ref[...]
    xs[half:, :] = other_ref[...]
    picked = dot(one_hot(slot, len(outs) * size), xs[...], ((0,), (0,)))
    for k, out_ref in enumerate(outs):
        out_ref[...] = picked[k * size:(k + 1) * size, :].astype(BF16)


def place_rows(n, spread_ref, w2_grad_ref, *refs):
    slots, (w2_grad_hbm, grad_ref, energy_ref, ys, sem) = refs[:n], refs[n:]
    copy = pltpu.make_async_copy(w2_grad_ref, w2_grad_hbm, sem)
    copy.start()
    width = grad_ref.shape[1]
    size = slots[0].shape[0]
    for k in range(n):
        ys[k * size:(k + 1) * size, :] = slots[k][...]
    grad_ref[...] = dot(spread_ref[...], ys[:, :width]).astype(BF16)
    energy_ref[...] = dot(ys[:, width:], spread_ref[...], ((0,), (1,)))[:1, :].astype(BF16)
    copy.wait()


def all_replicas(n, where_ref, *refs):
    slots = refs[:n]
    kept_ref, w1_ref, w2_ref, band_ref, readout_ref, w1_grad_hbm, w2_grad_ref = refs[n:n + 7]
    ys, hs, w1_grad_ref, sem = refs[n + 7:]
    size, kept = slots[0].shape[0], kept_ref.shape[0]
    width, hidden = w1_ref.shape
    band = band_ref.shape[1]
    new = n * size
    for k in range(n):
        ys[k * size:(k + 1) * size, :] = slots[k][...]
    ys[new:, :] = kept_ref[...]
    hs[new:, :] = band_ref[...]
    cot = ys[:new, width:].astype(F32)[:, 0:1]
    bands = hidden // band
    for j in range(bands):
        at = where_ref[1] + j
        at = jnp.where(at >= bands, at - bands, at)
        part = pl.ds(pl.multiple_of(at * band, band), band)
        preact = dot(ys[:new, :width], w1_ref[:, part])
        sig, act = gate(preact)
        w2_grad_ref[:, part] = readout_ref[:, part] + jnp.sum(cot * act, axis=0, keepdims=True)
        if j == 0:
            w2 = w2_ref[:, part].astype(F32)
            hs[:new, :] = (cot * w2 * sig * (1.0 + preact * (1.0 - sig))).astype(BF16)
            w1_grad_ref[...] = dot(hs[...], ys[:, :width], ((0,), (0,))).astype(BF16)
            copy = pltpu.make_async_copy(w1_grad_ref, w1_grad_hbm, sem)
            copy.start()
    copy.wait()


def by_blocks(descriptors, expert_ids, cotangent, w1, w2):
    owners, replicas = lax.axis_size("expert"), lax.axis_size("rep")
    rows, width = descriptors.shape
    wide = width + LANES
    hidden = w1.shape[2]
    band = hidden // replicas
    chips = owners // 2
    kept = owners * CAP
    where = jnp.stack([lax.axis_index("expert"), lax.axis_index("rep")]).astype(jnp.int32)

    def shape(*dims, dtype=BF16):
        return jax.ShapeDtypeStruct(dims, dtype)

    def to_chips(blocks):
        return [blocks[0]] + [swap(blocks[k], "expert", 2 * k) for k in range(1, chips)]

    begun = call(begin, shape(1, LANES, dtype=F32), (where,), flops=WAIT, scalars=1)
    own = call(
        label_rows, shape(rows, wide),
        (descriptors, expert_ids.reshape(1, rows), cotangent.reshape(1, rows), begun),
    )
    readout = w2
    weight = w1[0]
    far = [swap(own, "rep", k) for k in range(1, replicas)]
    far = call(stack_blocks, shape(len(far) * rows, wide), tuple(far), flops=WAIT)
    far_other = swap(far, "expert", 1)
    near = to_chips([own] * chips)
    near = call(stack_blocks, shape(chips * rows, wide), tuple(near), flops=WAIT)
    near_other = swap(near, "expert", 1)

    size = 2 * (replicas - 1) * CAP
    chosen = call(
        functools.partial(pick_slots, rows), [shape(size, wide)] * chips, (where, far, far_other),
        (pltpu.VMEM((2 * far.shape[0], wide), BF16),),
        flops=WAIT, scalars=1,
    )
    slots = to_chips(chosen)

    keep, give, band_grad, kept_rows, readout_part, spread = call(
        functools.partial(own_plane, chips, rows),
        [
            shape(kept // 2, wide), shape(kept // 2, wide), shape(kept, band), shape(kept, wide),
            shape(1, hidden, dtype=F32), shape(rows, kept),
        ],
        (where, near, near_other, weight, readout, chosen[0]),
        (pltpu.VMEM((owners * rows, wide), BF16), pltpu.VMEM((kept, hidden), BF16)),
        flops=4 * kept * width * hidden, scalars=1,
    )
    got = swap(give, "expert", 1)
    back = to_chips(call(join_cores, [shape(2 * CAP, wide)] * chips, (keep, got)))

    w1_grad, w2_grad = call(
        functools.partial(all_replicas, chips),
        (shape(band, width), shape(1, hidden, dtype=F32)),
        (where, *slots, kept_rows, weight, readout, band_grad, readout_part),
        (
            pltpu.VMEM((chips * size + kept, wide), BF16), pltpu.VMEM((chips * size + kept, band), BF16),
            pltpu.VMEM((band, width), BF16), DMA,
        ),
        flops=4 * WAIT, scalars=1, hbm_outs=1,
    )

    w2_grad, descriptor_grad, energies = call(
        functools.partial(place_rows, chips),
        (shape(1, hidden, dtype=F32), shape(rows, width), shape(1, rows)),
        (spread, w2_grad, *back), (pltpu.VMEM((kept, wide), BF16), DMA), hbm_outs=1,
    )
    return energies.reshape(rows), descriptor_grad, w1_grad[None], w2_grad


def by_slots(descriptors, expert_ids, cotangent, w1, w2):
    owners = lax.axis_size("expert")
    columns = descriptors.shape[1]
    slot_count = owners * CAP
    targets = expert_ids[:, 0]
    member = (targets[:, None] == jnp.arange(owners, dtype=jnp.int32)[None, :]).astype(jnp.int32)
    slot_rank = jnp.sum((jnp.cumsum(member, axis=0) - 1) * member, axis=1)
    placement = (
        (targets * CAP + slot_rank)[:, None] == jnp.arange(slot_count, dtype=jnp.int32)[None, :]
    ).astype(BF16)
    over_rows = ((0,), (0,))

    def exchange(slots):
        parted = slots.reshape(owners, CAP, *slots.shape[1:])
        moved = lax.all_to_all(parted, "expert", split_axis=0, concat_axis=0, tiled=True)
        return moved.reshape(slots.shape)

    slot_rows = exchange(dot(placement, descriptors, over_rows).astype(BF16))
    slot_cot = exchange(dot(placement, cotangent, over_rows).astype(BF16)).astype(F32)
    weight, readout = w1[0], w2[0].astype(F32)
    preact = dot(slot_rows, weight)
    sig = jax.nn.sigmoid(preact)
    activated = preact * sig
    energy = jnp.sum(activated * readout, axis=1).astype(BF16)
    hidden_grad = (slot_cot[:, None] * readout * sig * (1.0 + preact * (1.0 - sig))).astype(BF16)
    input_grad = dot(hidden_grad, weight, ((1,), (1,))).astype(BF16)
    energies = dot(placement, exchange(energy)).astype(BF16)
    descriptor_grad = dot(placement, exchange(input_grad)).astype(BF16)
    w2_grad = lax.psum(jnp.sum(slot_cot[:, None] * activated, axis=0), "rep")
    w1_grad = lax.psum_scatter(
        dot(hidden_grad, slot_rows, over_rows).astype(BF16), "rep", scatter_dimension=0, tiled=True
    )
    return energies, descriptor_grad, w1_grad[None], w2_grad[None]


def on_device(descriptors, *rest):
    few = descriptors.shape[0] * lax.axis_size("expert") <= PLANE_ROWS
    return (by_blocks if few else by_slots)(descriptors, *rest)


def solution(mesh):
    in_specs = (
        P(("expert", "rep"), None),
        P(("expert", "rep"), None),
        P(("expert", "rep")),
        P("expert", None, None),
        P("expert", None),
    )
    out_specs = (
        P(("expert", "rep")),
        P(("expert", "rep"), None),
        P("expert", "rep", None),
        P("expert", None),
    )
    return jax.shard_map(
        on_device, mesh=mesh, in_specs=in_specs, out_specs=out_specs, check_vma=False
    )
```

```python
import functools

import jax
import jax.numpy as jnp
from jax import lax
from jax.experimental import pallas as pl
from jax.experimental.pallas import tpu as pltpu
from jax.sharding import PartitionSpec as P

CAP = 12
LANES = 128
PLANE_ROWS = 512
WAIT = 5_000_000_000
F32, BF16 = jnp.float32, jnp.bfloat16
VMEM = pl.BlockSpec(memory_space=pltpu.VMEM)
SMEM = pl.BlockSpec(memory_space=pltpu.SMEM)
HBM = pl.BlockSpec(memory_space=pltpu.HBM)
DMA = pltpu.SemaphoreType.DMA


def call(kernel, out_shape, operands, scratch=(), flops=0, scalars=0, hbm_outs=0):
    outs = jax.tree.leaves(out_shape)
    specs = [HBM] * hbm_outs + [VMEM] * (len(outs) - hbm_outs)
    moved = sum(x.size * x.dtype.itemsize for x in jax.tree.leaves((out_shape, operands)))
    return pl.pallas_call(
        kernel,
        out_shape=out_shape,
        in_specs=[SMEM] * scalars + [VMEM] * (len(operands) - scalars),
        out_specs=jax.tree.unflatten(jax.tree.structure(out_shape), specs),
        scratch_shapes=list(scratch),
        cost_estimate=pl.CostEstimate(flops=flops, bytes_accessed=moved, transcendentals=0),
        compiler_params=pltpu.CompilerParams(vmem_limit_bytes=24 << 20),
    )(*operands)


def swap(x, axis, k):
    return lax.ppermute(x, axis, [(i, i ^ k) for i in range(lax.axis_size(axis))])


def iota(shape, dim):
    return lax.broadcasted_iota(jnp.int32, shape, dim)


def dot(a, b, dims=((1,), (0,))):
    return lax.dot_general(a, b, (dims, ((), ())), preferred_element_type=F32)


def begin(where_ref, token_ref):
    token_ref[...] = jnp.zeros(token_ref.shape, F32)


def label_rows(rows_ref, ids_ref, cot_ref, after_ref, out_ref):
    rows, width = rows_ref.shape
    i, j = iota((rows, rows), 0), iota((rows, rows), 1)

    def column(square):
        return jnp.sum(square, axis=1, keepdims=True)

    ids_line = jnp.broadcast_to(ids_ref[...].astype(F32), (rows, rows))
    cot_line = jnp.broadcast_to(cot_ref[...].astype(F32), (rows, rows))
    ids = column(jnp.where(i == j, ids_line, 0.0))
    cot = column(jnp.where(i == j, cot_line, 0.0))
    rank = column(jnp.where((j < i) & (ids_line == ids), 1.0, 0.0))
    for k in range(width // LANES):
        out_ref[k * rows:(k + 1) * rows, :] = rows_ref[:, k * LANES:(k + 1) * LANES]
    lane, groups = iota((8, LANES), 1), rows // 8
    tags = jnp.zeros((8, LANES), F32)
    for field, values in enumerate((cot, ids, rank)):
        for k in range(groups):
            tags = jnp.where(lane == field * groups + k, values[8 * k:8 * (k + 1), :], tags)
    out_ref[width // LANES * rows:, :] = tags.astype(BF16)


def stack_blocks(*refs):
    blocks, out_ref = refs[:-1], refs[-1]
    size = blocks[0].shape[0] - 8
    for k, block in enumerate(blocks):
        out_ref[k * size:(k + 1) * size, :] = block[:size, :]
    tags = jnp.concatenate([block[size:, :].astype(F32) for block in blocks], axis=0)
    out_ref[len(blocks) * size:, :] = tags.astype(BF16)


def unstack_blocks(rows, stacks, xs):
    width = xs.shape[1] - LANES
    tiles, groups = width // LANES, rows // 8
    tags, at = [], 0
    for stack in stacks:
        blocks = stack.shape[0] // (tiles * rows + 8)
        for b in range(blocks):
            for k in range(tiles):
                first = (b * tiles + k) * rows
                xs[at:at + rows, k * LANES:(k + 1) * LANES] = stack[first:first + rows, :]
            at += rows
        tags.append(stack[blocks * tiles * rows:, :].astype(F32))
    total = xs.shape[0]
    tags = jnp.concatenate([
        part[8 * b:8 * (b + 1), :] for part in tags for b in range(part.shape[0] // 8) for _ in range(groups)
    ], axis=0)
    lane, row = iota((total, LANES), 1), iota((total, LANES), 0)
    group = (row >> 3) & (groups - 1)

    def column(field):
        return jnp.sum(jnp.where(lane == field * groups + group, tags, 0.0), axis=1, keepdims=True)

    xs[:, width:] = jnp.where(lane == 0, column(0), 0.0).astype(BF16)
    return column(1).astype(jnp.int32), column(2).astype(jnp.int32)


def gate(preact):
    sig = 0.5 * jnp.tanh(0.5 * preact) + 0.5
    return sig, preact * sig


def first_slot(total, rows):
    return (iota((total, 1), 0) >> rows.bit_length() - 1) * CAP


def one_hot(slot, size):
    return jnp.where(slot == iota((slot.shape[0], size), 1), 1.0, 0.0).astype(BF16)


def own_plane(
    chips, rows, where_ref, near_ref, other_ref, w1_ref, w2_ref, after_ref,
    keep_ref, give_ref, band_ref, kept_ref, readout_ref, spread_ref, xs, hs,
):
    width, hidden = w1_ref.shape
    band = band_ref.shape[1]
    half = chips * rows
    kept = 2 * chips * CAP
    ids, ranks = unstack_blocks(rows, (near_ref, other_ref), xs)
    slot = jnp.where(ids == where_ref[0], first_slot(2 * half, rows) + ranks, -1)
    apart = ids[:rows] ^ where_ref[0]
    spread_ref[...] = one_hot((apart >> 1) * (2 * CAP) + (apart & 1) * CAP + ranks[:rows], kept)
    kept_ref[...] = dot(one_hot(slot, kept), xs[...], ((0,), (0,))).astype(BF16)
    cot = kept_ref[:, width:].astype(F32)[:, 0:1]
    energy = jnp.zeros((kept, 1), F32)
    for c in range(0, hidden, band):
        part = slice(c, c + band)
        preact = dot(kept_ref[:, :width], w1_ref[:, part])
        sig, act = gate(preact)
        w2 = w2_ref[:, part].astype(F32)
        energy += jnp.sum(act * w2, axis=1, keepdims=True)
        hs[:, part] = (cot * w2 * sig * (1.0 + preact * (1.0 - sig))).astype(BF16)
        readout_ref[:, part] = jnp.sum(cot * act, axis=0, keepdims=True)
    band_ref[...] = hs[:, pl.ds(pl.multiple_of(where_ref[1] * band, band), band)]
    back = dot(hs[...], w1_ref[...], ((1,), (1,)))
    tail = jnp.where(iota((kept, LANES), 1) == 0, energy, 0.0)
    for out_ref, part in ((keep_ref, slice(0, kept // 2)), (give_ref, slice(kept // 2, kept))):
        out_ref[:, :width] = back[part, :].astype(BF16)
        out_ref[:, width:] = tail[part, :].astype(BF16)


def join_cores(keep_ref, got_ref, *outs):
    keep, got = keep_ref[...].astype(F32), got_ref[...].astype(F32)
    for k, out_ref in enumerate(outs):
        part = slice(CAP * k, CAP * (k + 1))
        out_ref[...] = jnp.concatenate([keep[part, :], got[part, :]], axis=0).astype(BF16)


def pick_slots(rows, where_ref, far_ref, other_ref, *refs):
    outs, xs = refs[:-1], refs[-1]
    size = outs[0].shape[0]
    ids, ranks = unstack_blocks(rows, (far_ref, other_ref), xs)
    apart = ids ^ where_ref[0]
    slot = jnp.where(apart & 1 == 0, (apart >> 1) * size + first_slot(xs.shape[0], rows) + ranks, -1)
    picked = dot(one_hot(slot, len(outs) * size), xs[...], ((0,), (0,)))
    for k, out_ref in enumerate(outs):
        out_ref[...] = picked[k * size:(k + 1) * size, :].astype(BF16)


def place_rows(n, spread_ref, w2_grad_ref, *refs):
    slots, (w2_grad_hbm, grad_ref, energy_ref, ys, sem) = refs[:n], refs[n:]
    copy = pltpu.make_async_copy(w2_grad_ref, w2_grad_hbm, sem)
    copy.start()
    width = grad_ref.shape[1]
    size = slots[0].shape[0]
    for k in range(n):
        ys[k * size:(k + 1) * size, :] = slots[k][...]
    grad_ref[...] = dot(spread_ref[...], ys[:, :width]).astype(BF16)
    energy_ref[...] = dot(ys[:, width:], spread_ref[...], ((0,), (1,)))[:1, :].astype(BF16)
    copy.wait()


def all_replicas(n, where_ref, *refs):
    slots = refs[:n]
    kept_ref, w1_ref, w2_ref, band_ref, readout_ref, w1_grad_hbm, w2_grad_ref = refs[n:n + 7]
    ys, hs, w1_grad_ref, sem = refs[n + 7:]
    size, kept = slots[0].shape[0], kept_ref.shape[0]
    width, hidden = w1_ref.shape
    band = band_ref.shape[1]
    new = n * size
    for k in range(n):
        ys[k * size:(k + 1) * size, :] = slots[k][...]
    ys[new:, :] = kept_ref[...]
    hs[new:, :] = band_ref[...]
    cot = ys[:new, width:].astype(F32)[:, 0:1]
    bands = hidden // band
    for j in range(bands):
        at = where_ref[1] + j
        at = jnp.where(at >= bands, at - bands, at)
        part = pl.ds(pl.multiple_of(at * band, band), band)
        preact = dot(ys[:new, :width], w1_ref[:, part])
        sig, act = gate(preact)
        w2_grad_ref[:, part] = readout_ref[:, part] + jnp.sum(cot * act, axis=0, keepdims=True)
        if j == 0:
            w2 = w2_ref[:, part].astype(F32)
            hs[:new, :] = (cot * w2 * sig * (1.0 + preact * (1.0 - sig))).astype(BF16)
            w1_grad_ref[...] = dot(hs[...], ys[:, :width], ((0,), (0,))).astype(BF16)
            copy = pltpu.make_async_copy(w1_grad_ref, w1_grad_hbm, sem)
            copy.start()
    copy.wait()


def by_blocks(descriptors, expert_ids, cotangent, w1, w2):
    owners, replicas = lax.axis_size("expert"), lax.axis_size("rep")
    rows, width = descriptors.shape
    wide = width + LANES
    hidden = w1.shape[2]
    band = hidden // replicas
    chips = owners // 2
    kept = owners * CAP
    where = jnp.stack([lax.axis_index("expert"), lax.axis_index("rep")]).astype(jnp.int32)

    def shape(*dims, dtype=BF16):
        return jax.ShapeDtypeStruct(dims, dtype)

    def to_chips(blocks):
        return [blocks[0]] + [swap(blocks[k], "expert", 2 * k) for k in range(1, chips)]

    begun = call(begin, shape(1, LANES, dtype=F32), (where,), flops=WAIT, scalars=1)
    length = width // LANES * rows + 8
    own = call(
        label_rows, shape(length, LANES),
        (descriptors, expert_ids.reshape(1, rows), cotangent.reshape(1, rows), begun),
    )
    readout = w2
    weight = w1[0]
    far = [swap(own, "rep", k) for k in range(1, replicas)]
    far = call(stack_blocks, shape(len(far) * length, LANES), tuple(far), flops=WAIT)
    far_other = swap(far, "expert", 1)
    near = to_chips([own] * chips)
    near = call(stack_blocks, shape(chips * length, LANES), tuple(near), flops=WAIT)
    near_other = swap(near, "expert", 1)

    size = 2 * (replicas - 1) * CAP
    chosen = call(
        functools.partial(pick_slots, rows), [shape(size, wide)] * chips, (where, far, far_other),
        (pltpu.VMEM((2 * (replicas - 1) * rows, wide), BF16),),
        flops=WAIT, scalars=1,
    )
    slots = to_chips(chosen)

    keep, give, band_grad, kept_rows, readout_part, spread = call(
        functools.partial(own_plane, chips, rows),
        [
            shape(kept // 2, wide), shape(kept // 2, wide), shape(kept, band), shape(kept, wide),
            shape(1, hidden, dtype=F32), shape(rows, kept),
        ],
        (where, near, near_other, weight, readout, chosen[0]),
        (pltpu.VMEM((owners * rows, wide), BF16), pltpu.VMEM((kept, hidden), BF16)),
        flops=4 * kept * width * hidden, scalars=1,
    )
    got = swap(give, "expert", 1)
    back = to_chips(call(join_cores, [shape(2 * CAP, wide)] * chips, (keep, got)))

    w1_grad, w2_grad = call(
        functools.partial(all_replicas, chips),
        (shape(band, width), shape(1, hidden, dtype=F32)),
        (where, *slots, kept_rows, weight, readout, band_grad, readout_part),
        (
            pltpu.VMEM((chips * size + kept, wide), BF16), pltpu.VMEM((chips * size + kept, band), BF16),
            pltpu.VMEM((band, width), BF16), DMA,
        ),
        flops=4 * WAIT, scalars=1, hbm_outs=1,
    )

    w2_grad, descriptor_grad, energies = call(
        functools.partial(place_rows, chips),
        (shape(1, hidden, dtype=F32), shape(rows, width), shape(1, rows)),
        (spread, w2_grad, *back), (pltpu.VMEM((kept, wide), BF16), DMA), hbm_outs=1,
    )
    return energies.reshape(rows), descriptor_grad, w1_grad[None], w2_grad


def by_slots(descriptors, expert_ids, cotangent, w1, w2):
    owners = lax.axis_size("expert")
    columns = descriptors.shape[1]
    slot_count = owners * CAP
    targets = expert_ids[:, 0]
    member = (targets[:, None] == jnp.arange(owners, dtype=jnp.int32)[None, :]).astype(jnp.int32)
    slot_rank = jnp.sum((jnp.cumsum(member, axis=0) - 1) * member, axis=1)
    placement = (
        (targets * CAP + slot_rank)[:, None] == jnp.arange(slot_count, dtype=jnp.int32)[None, :]
    ).astype(BF16)
    over_rows = ((0,), (0,))

    def exchange(slots):
        parted = slots.reshape(owners, CAP, *slots.shape[1:])
        moved = lax.all_to_all(parted, "expert", split_axis=0, concat_axis=0, tiled=True)
        return moved.reshape(slots.shape)

    slot_rows = exchange(dot(placement, descriptors, over_rows).astype(BF16))
    slot_cot = exchange(dot(placement, cotangent, over_rows).astype(BF16)).astype(F32)
    weight, readout = w1[0], w2[0].astype(F32)
    preact = dot(slot_rows, weight)
    sig = jax.nn.sigmoid(preact)
    activated = preact * sig
    energy = jnp.sum(activated * readout, axis=1).astype(BF16)
    hidden_grad = (slot_cot[:, None] * readout * sig * (1.0 + preact * (1.0 - sig))).astype(BF16)
    input_grad = dot(hidden_grad, weight, ((1,), (1,))).astype(BF16)
    energies = dot(placement, exchange(energy)).astype(BF16)
    descriptor_grad = dot(placement, exchange(input_grad)).astype(BF16)
    w2_grad = lax.psum(jnp.sum(slot_cot[:, None] * activated, axis=0), "rep")
    w1_grad = lax.psum_scatter(
        dot(hidden_grad, slot_rows, over_rows).astype(BF16), "rep", scatter_dimension=0, tiled=True
    )
    return energies, descriptor_grad, w1_grad[None], w2_grad[None]


def on_device(descriptors, *rest):
    few = descriptors.shape[0] * lax.axis_size("expert") <= PLANE_ROWS
    return (by_blocks if few else by_slots)(descriptors, *rest)


def solution(mesh):
    in_specs = (
        P(("expert", "rep"), None),
        P(("expert", "rep"), None),
        P(("expert", "rep")),
        P("expert", None, None),
        P("expert", None),
    )
    out_specs = (
        P(("expert", "rep")),
        P(("expert", "rep"), None),
        P("expert", "rep", None),
        P("expert", None),
    )
    return jax.shard_map(
        on_device, mesh=mesh, in_specs=in_specs, out_specs=out_specs, check_vma=False
    )
```

```python
import functools

import jax
import jax.numpy as jnp
from jax import lax
from jax.experimental import pallas as pl
from jax.experimental.pallas import tpu as pltpu
from jax.sharding import PartitionSpec as P

CAP = 12
LANES = 128
PLANE_ROWS = 512
WAIT = 5_000_000_000
F32, BF16 = jnp.float32, jnp.bfloat16
VMEM = pl.BlockSpec(memory_space=pltpu.VMEM)
SMEM = pl.BlockSpec(memory_space=pltpu.SMEM)
HBM = pl.BlockSpec(memory_space=pltpu.HBM)
DMA = pltpu.SemaphoreType.DMA


def call(kernel, out_shape, operands, scratch=(), flops=0, scalars=0, hbm_outs=0):
    outs = jax.tree.leaves(out_shape)
    specs = [HBM] * hbm_outs + [VMEM] * (len(outs) - hbm_outs)
    moved = sum(x.size * x.dtype.itemsize for x in jax.tree.leaves((out_shape, operands)))
    return pl.pallas_call(
        kernel,
        out_shape=out_shape,
        in_specs=[SMEM] * scalars + [VMEM] * (len(operands) - scalars),
        out_specs=jax.tree.unflatten(jax.tree.structure(out_shape), specs),
        scratch_shapes=list(scratch),
        cost_estimate=pl.CostEstimate(flops=flops, bytes_accessed=moved, transcendentals=0),
        compiler_params=pltpu.CompilerParams(vmem_limit_bytes=24 << 20),
    )(*operands)


def swap(x, axis, k):
    return lax.ppermute(x, axis, [(i, i ^ k) for i in range(lax.axis_size(axis))])


def iota(shape, dim):
    return lax.broadcasted_iota(jnp.int32, shape, dim)


def dot(a, b, dims=((1,), (0,))):
    return lax.dot_general(a, b, (dims, ((), ())), preferred_element_type=F32)


def begin(where_ref, token_ref):
    token_ref[...] = jnp.zeros(token_ref.shape, F32)


def label_rows(rows_ref, ids_ref, cot_ref, after_ref, out_ref):
    rows, width = rows_ref.shape
    i, j = iota((rows, rows), 0), iota((rows, rows), 1)

    def column(square):
        return jnp.sum(square, axis=1, keepdims=True)

    ids_line = jnp.broadcast_to(ids_ref[...].astype(F32), (rows, rows))
    cot_line = jnp.broadcast_to(cot_ref[...].astype(F32), (rows, rows))
    ids = column(jnp.where(i == j, ids_line, 0.0))
    cot = column(jnp.where(i == j, cot_line, 0.0))
    rank = column(jnp.where((j < i) & (ids_line == ids), 1.0, 0.0))
    for k in range(width // LANES):
        out_ref[k * rows:(k + 1) * rows, :] = rows_ref[:, k * LANES:(k + 1) * LANES]
    lane, groups = iota((8, LANES), 1), rows // 8
    tags = jnp.zeros((8, LANES), F32)
    for field, values in enumerate((cot, ids, rank)):
        for k in range(groups):
            tags = jnp.where(lane == field * groups + k, values[8 * k:8 * (k + 1), :], tags)
    out_ref[width // LANES * rows:, :] = tags.astype(BF16)


def stack_blocks(*refs):
    blocks, out_ref = refs[:-1], refs[-1]
    size = blocks[0].shape[0] - 8
    for k, block in enumerate(blocks):
        out_ref[k * size:(k + 1) * size, :] = block[:size, :]
    tags = jnp.concatenate([block[size:, :].astype(F32) for block in blocks], axis=0)
    out_ref[len(blocks) * size:, :] = tags.astype(BF16)


def unstack_blocks(rows, stacks, xs):
    width = xs.shape[1] - LANES
    tiles, groups = width // LANES, rows // 8
    tags, at = [], 0
    for stack in stacks:
        blocks = stack.shape[0] // (tiles * rows + 8)
        for b in range(blocks):
            for k in range(tiles):
                first = (b * tiles + k) * rows
                xs[at:at + rows, k * LANES:(k + 1) * LANES] = stack[first:first + rows, :]
            at += rows
        tags.append(stack[blocks * tiles * rows:, :].astype(F32))
    total = xs.shape[0]
    tags = jnp.concatenate([
        part[8 * b:8 * (b + 1), :] for part in tags for b in range(part.shape[0] // 8) for _ in range(groups)
    ], axis=0)
    lane, row = iota((total, LANES), 1), iota((total, LANES), 0)
    group = (row >> 3) & (groups - 1)

    def column(field):
        return jnp.sum(jnp.where(lane == field * groups + group, tags, 0.0), axis=1, keepdims=True)

    xs[:, width:] = jnp.where(lane == 0, column(0), 0.0).astype(BF16)
    return column(1).astype(jnp.int32), column(2).astype(jnp.int32)


def gate(preact):
    sig = 0.5 * jnp.tanh(0.5 * preact) + 0.5
    return sig, preact * sig


def first_slot(total, rows):
    return (iota((total, 1), 0) >> rows.bit_length() - 1) * CAP


def partner_and_side(apart):
    return apart >> 1, jnp.where(apart > 1, (apart & 1) ^ 1, apart)


def one_hot(slot, size):
    return jnp.where(slot == iota((slot.shape[0], size), 1), 1.0, 0.0).astype(BF16)


def own_plane(
    chips, rows, where_ref, near_ref, other_ref, w1_ref, w2_ref, after_ref,
    keep_ref, give_ref, band_ref, kept_ref, readout_ref, spread_ref, xs, hs,
):
    width, hidden = w1_ref.shape
    band = band_ref.shape[1]
    half = chips * rows
    kept = 2 * chips * CAP
    ids, ranks = unstack_blocks(rows, (near_ref, other_ref), xs)
    slot = jnp.where(ids == where_ref[0], first_slot(2 * half, rows) + ranks, -1)
    apart = ids[:rows] ^ where_ref[0]
    chip, side = partner_and_side(apart)
    spread_ref[...] = one_hot(chip * (2 * CAP) + side * CAP + ranks[:rows], kept)
    kept_ref[...] = dot(one_hot(slot, kept), xs[...], ((0,), (0,))).astype(BF16)
    cot = kept_ref[:, width:].astype(F32)[:, 0:1]
    energy = jnp.zeros((kept, 1), F32)
    for c in range(0, hidden, band):
        part = slice(c, c + band)
        preact = dot(kept_ref[:, :width], w1_ref[:, part])
        sig, act = gate(preact)
        w2 = w2_ref[:, part].astype(F32)
        energy += jnp.sum(act * w2, axis=1, keepdims=True)
        hs[:, part] = (cot * w2 * sig * (1.0 + preact * (1.0 - sig))).astype(BF16)
        readout_ref[:, part] = jnp.sum(cot * act, axis=0, keepdims=True)
    band_ref[...] = hs[:, pl.ds(pl.multiple_of(where_ref[1] * band, band), band)]
    back = dot(hs[...], w1_ref[...], ((1,), (1,)))
    tail = jnp.where(iota((kept, LANES), 1) == 0, energy, 0.0)
    for out_ref, part in ((keep_ref, slice(0, kept // 2)), (give_ref, slice(kept // 2, kept))):
        out_ref[:, :width] = back[part, :].astype(BF16)
        out_ref[:, width:] = tail[part, :].astype(BF16)


def join_cores(keep_ref, got_ref, *outs):
    keep, got = keep_ref[...].astype(F32), got_ref[...].astype(F32)
    for k, out_ref in enumerate(outs):
        part = slice(CAP * k, CAP * (k + 1))
        out_ref[...] = jnp.concatenate([keep[part, :], got[part, :]], axis=0).astype(BF16)


def pick_slots(rows, where_ref, far_ref, other_ref, *refs):
    outs, xs = refs[:-1], refs[-1]
    size = outs[0].shape[0]
    ids, ranks = unstack_blocks(rows, (far_ref, other_ref), xs)
    apart = ids ^ where_ref[0]
    chip, side = partner_and_side(apart)
    slot = jnp.where(side == 0, chip * size + first_slot(xs.shape[0], rows) + ranks, -1)
    picked = dot(one_hot(slot, len(outs) * size), xs[...], ((0,), (0,)))
    for k, out_ref in enumerate(outs):
        out_ref[...] = picked[k * size:(k + 1) * size, :].astype(BF16)


def place_rows(n, spread_ref, w2_grad_ref, *refs):
    slots, (w2_grad_hbm, grad_ref, energy_ref, ys, sem) = refs[:n], refs[n:]
    copy = pltpu.make_async_copy(w2_grad_ref, w2_grad_hbm, sem)
    copy.start()
    width = grad_ref.shape[1]
    size = slots[0].shape[0]
    for k in range(n):
        ys[k * size:(k + 1) * size, :] = slots[k][...]
    grad_ref[...] = dot(spread_ref[...], ys[:, :width]).astype(BF16)
    energy_ref[...] = dot(ys[:, width:], spread_ref[...], ((0,), (1,)))[:1, :].astype(BF16)
    copy.wait()


def all_replicas(n, where_ref, *refs):
    slots = refs[:n]
    kept_ref, w1_ref, w2_ref, band_ref, readout_ref, w1_grad_hbm, w2_grad_ref = refs[n:n + 7]
    ys, hs, w1_grad_ref, sem = refs[n + 7:]
    size, kept = slots[0].shape[0], kept_ref.shape[0]
    width, hidden = w1_ref.shape
    band = band_ref.shape[1]
    new = n * size
    for k in range(n):
        ys[k * size:(k + 1) * size, :] = slots[k][...]
    ys[new:, :] = kept_ref[...]
    hs[new:, :] = band_ref[...]
    cot = ys[:new, width:].astype(F32)[:, 0:1]
    bands = hidden // band
    for j in range(bands):
        at = where_ref[1] + j
        at = jnp.where(at >= bands, at - bands, at)
        part = pl.ds(pl.multiple_of(at * band, band), band)
        preact = dot(ys[:new, :width], w1_ref[:, part])
        sig, act = gate(preact)
        w2_grad_ref[:, part] = readout_ref[:, part] + jnp.sum(cot * act, axis=0, keepdims=True)
        if j == 0:
            w2 = w2_ref[:, part].astype(F32)
            hs[:new, :] = (cot * w2 * sig * (1.0 + preact * (1.0 - sig))).astype(BF16)
            w1_grad_ref[...] = dot(hs[...], ys[:, :width], ((0,), (0,))).astype(BF16)
            copy = pltpu.make_async_copy(w1_grad_ref, w1_grad_hbm, sem)
            copy.start()
    copy.wait()


def by_blocks(descriptors, expert_ids, cotangent, w1, w2):
    owners, replicas = lax.axis_size("expert"), lax.axis_size("rep")
    rows, width = descriptors.shape
    wide = width + LANES
    hidden = w1.shape[2]
    band = hidden // replicas
    chips = owners // 2
    kept = owners * CAP
    where = jnp.stack([lax.axis_index("expert"), lax.axis_index("rep")]).astype(jnp.int32)

    def shape(*dims, dtype=BF16):
        return jax.ShapeDtypeStruct(dims, dtype)

    def to_chips(blocks):
        return [blocks[0]] + [swap(blocks[k], "expert", 2 * k + 1) for k in range(1, chips)]

    begun = call(begin, shape(1, LANES, dtype=F32), (where,), flops=WAIT, scalars=1)
    length = width // LANES * rows + 8
    own = call(
        label_rows, shape(length, LANES),
        (descriptors, expert_ids.reshape(1, rows), cotangent.reshape(1, rows), begun),
    )
    readout = w2
    weight = w1[0]
    far = [swap(own, "rep", k) for k in range(1, replicas)]
    far = call(stack_blocks, shape(len(far) * length, LANES), tuple(far), flops=WAIT)
    far_other = swap(far, "expert", 1)
    near = to_chips([own] * chips)
    near = call(stack_blocks, shape(chips * length, LANES), tuple(near), flops=WAIT)
    near_other = swap(near, "expert", 1)

    size = 2 * (replicas - 1) * CAP
    chosen = call(
        functools.partial(pick_slots, rows), [shape(size, wide)] * chips, (where, far, far_other),
        (pltpu.VMEM((2 * (replicas - 1) * rows, wide), BF16),),
        flops=WAIT, scalars=1,
    )
    slots = to_chips(chosen)

    keep, give, band_grad, kept_rows, readout_part, spread = call(
        functools.partial(own_plane, chips, rows),
        [
            shape(kept // 2, wide), shape(kept // 2, wide), shape(kept, band), shape(kept, wide),
            shape(1, hidden, dtype=F32), shape(rows, kept),
        ],
        (where, near, near_other, weight, readout, chosen[0]),
        (pltpu.VMEM((owners * rows, wide), BF16), pltpu.VMEM((kept, hidden), BF16)),
        flops=4 * kept * width * hidden, scalars=1,
    )
    got = swap(give, "expert", 1)
    back = to_chips(call(join_cores, [shape(2 * CAP, wide)] * chips, (keep, got)))

    w1_grad, w2_grad = call(
        functools.partial(all_replicas, chips),
        (shape(band, width), shape(1, hidden, dtype=F32)),
        (where, *slots, kept_rows, weight, readout, band_grad, readout_part),
        (
            pltpu.VMEM((chips * size + kept, wide), BF16), pltpu.VMEM((chips * size + kept, band), BF16),
            pltpu.VMEM((band, width), BF16), DMA,
        ),
        flops=4 * WAIT, scalars=1, hbm_outs=1,
    )

    w2_grad, descriptor_grad, energies = call(
        functools.partial(place_rows, chips),
        (shape(1, hidden, dtype=F32), shape(rows, width), shape(1, rows)),
        (spread, w2_grad, *back), (pltpu.VMEM((kept, wide), BF16), DMA), hbm_outs=1,
    )
    return energies.reshape(rows), descriptor_grad, w1_grad[None], w2_grad


def by_slots(descriptors, expert_ids, cotangent, w1, w2):
    owners = lax.axis_size("expert")
    columns = descriptors.shape[1]
    slot_count = owners * CAP
    targets = expert_ids[:, 0]
    member = (targets[:, None] == jnp.arange(owners, dtype=jnp.int32)[None, :]).astype(jnp.int32)
    slot_rank = jnp.sum((jnp.cumsum(member, axis=0) - 1) * member, axis=1)
    placement = (
        (targets * CAP + slot_rank)[:, None] == jnp.arange(slot_count, dtype=jnp.int32)[None, :]
    ).astype(BF16)
    over_rows = ((0,), (0,))

    def exchange(slots):
        parted = slots.reshape(owners, CAP, *slots.shape[1:])
        moved = lax.all_to_all(parted, "expert", split_axis=0, concat_axis=0, tiled=True)
        return moved.reshape(slots.shape)

    slot_rows = exchange(dot(placement, descriptors, over_rows).astype(BF16))
    slot_cot = exchange(dot(placement, cotangent, over_rows).astype(BF16)).astype(F32)
    weight, readout = w1[0], w2[0].astype(F32)
    preact = dot(slot_rows, weight)
    sig = jax.nn.sigmoid(preact)
    activated = preact * sig
    energy = jnp.sum(activated * readout, axis=1).astype(BF16)
    hidden_grad = (slot_cot[:, None] * readout * sig * (1.0 + preact * (1.0 - sig))).astype(BF16)
    input_grad = dot(hidden_grad, weight, ((1,), (1,))).astype(BF16)
    energies = dot(placement, exchange(energy)).astype(BF16)
    descriptor_grad = dot(placement, exchange(input_grad)).astype(BF16)
    w2_grad = lax.psum(jnp.sum(slot_cot[:, None] * activated, axis=0), "rep")
    w1_grad = lax.psum_scatter(
        dot(hidden_grad, slot_rows, over_rows).astype(BF16), "rep", scatter_dimension=0, tiled=True
    )
    return energies, descriptor_grad, w1_grad[None], w2_grad[None]


def on_device(descriptors, *rest):
    few = descriptors.shape[0] * lax.axis_size("expert") <= PLANE_ROWS
    return (by_blocks if few else by_slots)(descriptors, *rest)


def solution(mesh):
    in_specs = (
        P(("expert", "rep"), None),
        P(("expert", "rep"), None),
        P(("expert", "rep")),
        P("expert", None, None),
        P("expert", None),
    )
    out_specs = (
        P(("expert", "rep")),
        P(("expert", "rep"), None),
        P("expert", "rep", None),
        P("expert", None),
    )
    return jax.shard_map(
        on_device, mesh=mesh, in_specs=in_specs, out_specs=out_specs, check_vma=False
    )
```

```python
import functools

import jax
import jax.numpy as jnp
from jax import lax
from jax.experimental import pallas as pl
from jax.experimental.pallas import tpu as pltpu
from jax.sharding import PartitionSpec as P

CAP = 12
CROSSED_CHIPS = 0b1100
CROSSED_REPLICAS = 0b100
LANES = 128
PLANE_ROWS = 512
WAIT = 5_000_000_000
F32, BF16 = jnp.float32, jnp.bfloat16
VMEM = pl.BlockSpec(memory_space=pltpu.VMEM)
SMEM = pl.BlockSpec(memory_space=pltpu.SMEM)
HBM = pl.BlockSpec(memory_space=pltpu.HBM)
DMA = pltpu.SemaphoreType.DMA


def call(kernel, out_shape, operands, scratch=(), flops=0, scalars=0, hbm_outs=0):
    outs = jax.tree.leaves(out_shape)
    specs = [HBM] * hbm_outs + [VMEM] * (len(outs) - hbm_outs)
    moved = sum(x.size * x.dtype.itemsize for x in jax.tree.leaves((out_shape, operands)))
    return pl.pallas_call(
        kernel,
        out_shape=out_shape,
        in_specs=[SMEM] * scalars + [VMEM] * (len(operands) - scalars),
        out_specs=jax.tree.unflatten(jax.tree.structure(out_shape), specs),
        scratch_shapes=list(scratch),
        cost_estimate=pl.CostEstimate(flops=flops, bytes_accessed=moved, transcendentals=0),
        compiler_params=pltpu.CompilerParams(vmem_limit_bytes=24 << 20),
    )(*operands)


def swap(x, axis, k):
    return lax.ppermute(x, axis, [(i, i ^ k) for i in range(lax.axis_size(axis))])


def iota(shape, dim):
    return lax.broadcasted_iota(jnp.int32, shape, dim)


def dot(a, b, dims=((1,), (0,))):
    return lax.dot_general(a, b, (dims, ((), ())), preferred_element_type=F32)


def begin(where_ref, token_ref):
    token_ref[...] = jnp.zeros(token_ref.shape, F32)


def label_rows(rows_ref, ids_ref, cot_ref, after_ref, out_ref):
    rows, width = rows_ref.shape
    i, j = iota((rows, rows), 0), iota((rows, rows), 1)

    def column(square):
        return jnp.sum(square, axis=1, keepdims=True)

    ids_line = jnp.broadcast_to(ids_ref[...].astype(F32), (rows, rows))
    cot_line = jnp.broadcast_to(cot_ref[...].astype(F32), (rows, rows))
    ids = column(jnp.where(i == j, ids_line, 0.0))
    cot = column(jnp.where(i == j, cot_line, 0.0))
    rank = column(jnp.where((j < i) & (ids_line == ids), 1.0, 0.0))
    for k in range(width // LANES):
        out_ref[k * rows:(k + 1) * rows, :] = rows_ref[:, k * LANES:(k + 1) * LANES]
    lane, groups = iota((8, LANES), 1), rows // 8
    tags = jnp.zeros((8, LANES), F32)
    for field, values in enumerate((cot, ids, rank)):
        for k in range(groups):
            tags = jnp.where(lane == field * groups + k, values[8 * k:8 * (k + 1), :], tags)
    out_ref[width // LANES * rows:, :] = tags.astype(BF16)


def stack_blocks(*refs):
    blocks, out_ref = refs[:-1], refs[-1]
    size = blocks[0].shape[0] - 8
    for k, block in enumerate(blocks):
        out_ref[k * size:(k + 1) * size, :] = block[:size, :]
    tags = jnp.concatenate([block[size:, :].astype(F32) for block in blocks], axis=0)
    out_ref[len(blocks) * size:, :] = tags.astype(BF16)


def unstack_blocks(rows, stacks, xs):
    width = xs.shape[1] - LANES
    tiles, groups = width // LANES, rows // 8
    tags, at = [], 0
    for stack in stacks:
        blocks = stack.shape[0] // (tiles * rows + 8)
        for b in range(blocks):
            for k in range(tiles):
                first = (b * tiles + k) * rows
                xs[at:at + rows, k * LANES:(k + 1) * LANES] = stack[first:first + rows, :]
            at += rows
        tags.append(stack[blocks * tiles * rows:, :].astype(F32))
    total = xs.shape[0]
    tags = jnp.concatenate([
        part[8 * b:8 * (b + 1), :] for part in tags for b in range(part.shape[0] // 8) for _ in range(groups)
    ], axis=0)
    lane, row = iota((total, LANES), 1), iota((total, LANES), 0)
    group = (row >> 3) & (groups - 1)

    def column(field):
        return jnp.sum(jnp.where(lane == field * groups + group, tags, 0.0), axis=1, keepdims=True)

    xs[:, width:] = jnp.where(lane == 0, column(0), 0.0).astype(BF16)
    return column(1).astype(jnp.int32), column(2).astype(jnp.int32)


def gate(preact):
    sig = 0.5 * jnp.tanh(0.5 * preact) + 0.5
    return sig, preact * sig


def first_slot(total, rows):
    return (iota((total, 1), 0) >> rows.bit_length() - 1) * CAP


def partner_and_side(apart):
    return apart >> 1, (apart & 1) ^ (CROSSED_CHIPS >> (apart >> 1) & 1)


def one_hot(slot, size):
    return jnp.where(slot == iota((slot.shape[0], size), 1), 1.0, 0.0).astype(BF16)


def own_plane(
    chips, rows, where_ref, near_ref, other_ref, w1_ref, w2_ref, after_ref,
    keep_ref, give_ref, band_ref, kept_ref, readout_ref, spread_ref, xs, hs,
):
    width, hidden = w1_ref.shape
    band = band_ref.shape[1]
    half = chips * rows
    kept = 2 * chips * CAP
    ids, ranks = unstack_blocks(rows, (near_ref, other_ref), xs)
    slot = jnp.where(ids == where_ref[0], first_slot(2 * half, rows) + ranks, -1)
    apart = ids[:rows] ^ where_ref[0]
    chip, side = partner_and_side(apart)
    spread_ref[...] = one_hot(chip * (2 * CAP) + side * CAP + ranks[:rows], kept)
    kept_ref[...] = dot(one_hot(slot, kept), xs[...], ((0,), (0,))).astype(BF16)
    cot = kept_ref[:, width:].astype(F32)[:, 0:1]
    energy = jnp.zeros((kept, 1), F32)
    for c in range(0, hidden, band):
        part = slice(c, c + band)
        preact = dot(kept_ref[:, :width], w1_ref[:, part])
        sig, act = gate(preact)
        w2 = w2_ref[:, part].astype(F32)
        energy += jnp.sum(act * w2, axis=1, keepdims=True)
        hs[:, part] = (cot * w2 * sig * (1.0 + preact * (1.0 - sig))).astype(BF16)
        readout_ref[:, part] = jnp.sum(cot * act, axis=0, keepdims=True)
    band_ref[...] = hs[:, pl.ds(pl.multiple_of(where_ref[1] * band, band), band)]
    back = dot(hs[...], w1_ref[...], ((1,), (1,)))
    tail = jnp.where(iota((kept, LANES), 1) == 0, energy, 0.0)
    for out_ref, part in ((keep_ref, slice(0, kept // 2)), (give_ref, slice(kept // 2, kept))):
        out_ref[:, :width] = back[part, :].astype(BF16)
        out_ref[:, width:] = tail[part, :].astype(BF16)


def join_cores(keep_ref, got_ref, *outs):
    keep, got = keep_ref[...].astype(F32), got_ref[...].astype(F32)
    for k, out_ref in enumerate(outs):
        part = slice(CAP * k, CAP * (k + 1))
        out_ref[...] = jnp.concatenate([keep[part, :], got[part, :]], axis=0).astype(BF16)


def pick_slots(rows, where_ref, far_ref, other_ref, *refs):
    outs, xs = refs[:-1], refs[-1]
    size = outs[0].shape[0]
    ids, ranks = unstack_blocks(rows, (far_ref, other_ref), xs)
    apart = ids ^ where_ref[0]
    chip, side = partner_and_side(apart)
    slot = jnp.where(side == 0, chip * size + first_slot(xs.shape[0], rows) + ranks, -1)
    picked = dot(one_hot(slot, len(outs) * size), xs[...], ((0,), (0,)))
    for k, out_ref in enumerate(outs):
        out_ref[...] = picked[k * size:(k + 1) * size, :].astype(BF16)


def place_rows(n, spread_ref, w2_grad_ref, *refs):
    slots, (w2_grad_hbm, grad_ref, energy_ref, ys, sem) = refs[:n], refs[n:]
    copy = pltpu.make_async_copy(w2_grad_ref, w2_grad_hbm, sem)
    copy.start()
    width = grad_ref.shape[1]
    size = slots[0].shape[0]
    for k in range(n):
        ys[k * size:(k + 1) * size, :] = slots[k][...]
    grad_ref[...] = dot(spread_ref[...], ys[:, :width]).astype(BF16)
    energy_ref[...] = dot(ys[:, width:], spread_ref[...], ((0,), (1,)))[:1, :].astype(BF16)
    copy.wait()


def all_replicas(n, where_ref, *refs):
    slots = refs[:n]
    kept_ref, w1_ref, w2_ref, band_ref, readout_ref, w1_grad_hbm, w2_grad_ref = refs[n:n + 7]
    ys, hs, w1_grad_ref, sem = refs[n + 7:]
    size, kept = slots[0].shape[0], kept_ref.shape[0]
    width, hidden = w1_ref.shape
    band = band_ref.shape[1]
    new = n * size
    for k in range(n):
        ys[k * size:(k + 1) * size, :] = slots[k][...]
    ys[new:, :] = kept_ref[...]
    hs[new:, :] = band_ref[...]
    cot = ys[:new, width:].astype(F32)[:, 0:1]
    bands = hidden // band
    for j in range(bands):
        at = where_ref[1] + j
        at = jnp.where(at >= bands, at - bands, at)
        part = pl.ds(pl.multiple_of(at * band, band), band)
        preact = dot(ys[:new, :width], w1_ref[:, part])
        sig, act = gate(preact)
        w2_grad_ref[:, part] = readout_ref[:, part] + jnp.sum(cot * act, axis=0, keepdims=True)
        if j == 0:
            w2 = w2_ref[:, part].astype(F32)
            hs[:new, :] = (cot * w2 * sig * (1.0 + preact * (1.0 - sig))).astype(BF16)
            w1_grad_ref[...] = dot(hs[...], ys[:, :width], ((0,), (0,))).astype(BF16)
            copy = pltpu.make_async_copy(w1_grad_ref, w1_grad_hbm, sem)
            copy.start()
    copy.wait()


def by_blocks(descriptors, expert_ids, cotangent, w1, w2):
    owners, replicas = lax.axis_size("expert"), lax.axis_size("rep")
    rows, width = descriptors.shape
    wide = width + LANES
    hidden = w1.shape[2]
    band = hidden // replicas
    chips = owners // 2
    kept = owners * CAP
    where = jnp.stack([lax.axis_index("expert"), lax.axis_index("rep")]).astype(jnp.int32)

    def shape(*dims, dtype=BF16):
        return jax.ShapeDtypeStruct(dims, dtype)

    def to_chips(blocks):
        return [blocks[0]] + [swap(blocks[k], "expert", 2 * k + (CROSSED_CHIPS >> k & 1)) for k in range(1, chips)]

    begun = call(begin, shape(1, LANES, dtype=F32), (where,), flops=WAIT, scalars=1)
    length = width // LANES * rows + 8
    own = call(
        label_rows, shape(length, LANES),
        (descriptors, expert_ids.reshape(1, rows), cotangent.reshape(1, rows), begun),
    )
    readout = w2
    weight = w1[0]
    far = [swap(own, ("expert", "rep"), replicas * (CROSSED_REPLICAS >> k & 1) + k) for k in range(1, replicas)]
    far = call(stack_blocks, shape(len(far) * length, LANES), tuple(far), flops=WAIT)
    far_other = swap(far, "expert", 1)
    near = to_chips([own] * chips)
    near = call(stack_blocks, shape(chips * length, LANES), tuple(near), flops=WAIT)
    near_other = swap(near, "expert", 1)

    size = 2 * (replicas - 1) * CAP
    chosen = call(
        functools.partial(pick_slots, rows), [shape(size, wide)] * chips, (where, far, far_other),
        (pltpu.VMEM((2 * (replicas - 1) * rows, wide), BF16),),
        flops=WAIT, scalars=1,
    )
    slots = to_chips(chosen)

    keep, give, band_grad, kept_rows, readout_part, spread = call(
        functools.partial(own_plane, chips, rows),
        [
            shape(kept // 2, wide), shape(kept // 2, wide), shape(kept, band), shape(kept, wide),
            shape(1, hidden, dtype=F32), shape(rows, kept),
        ],
        (where, near, near_other, weight, readout, chosen[0]),
        (pltpu.VMEM((owners * rows, wide), BF16), pltpu.VMEM((kept, hidden), BF16)),
        flops=4 * kept * width * hidden, scalars=1,
    )
    got = swap(give, "expert", 1)
    back = to_chips(call(join_cores, [shape(2 * CAP, wide)] * chips, (keep, got)))

    w1_grad, w2_grad = call(
        functools.partial(all_replicas, chips),
        (shape(band, width), shape(1, hidden, dtype=F32)),
        (where, *slots, kept_rows, weight, readout, band_grad, readout_part),
        (
            pltpu.VMEM((chips * size + kept, wide), BF16), pltpu.VMEM((chips * size + kept, band), BF16),
            pltpu.VMEM((band, width), BF16), DMA,
        ),
        flops=4 * WAIT, scalars=1, hbm_outs=1,
    )

    w2_grad, descriptor_grad, energies = call(
        functools.partial(place_rows, chips),
        (shape(1, hidden, dtype=F32), shape(rows, width), shape(1, rows)),
        (spread, w2_grad, *back), (pltpu.VMEM((kept, wide), BF16), DMA), hbm_outs=1,
    )
    return energies.reshape(rows), descriptor_grad, w1_grad[None], w2_grad


def by_slots(descriptors, expert_ids, cotangent, w1, w2):
    owners = lax.axis_size("expert")
    columns = descriptors.shape[1]
    slot_count = owners * CAP
    targets = expert_ids[:, 0]
    member = (targets[:, None] == jnp.arange(owners, dtype=jnp.int32)[None, :]).astype(jnp.int32)
    slot_rank = jnp.sum((jnp.cumsum(member, axis=0) - 1) * member, axis=1)
    placement = (
        (targets * CAP + slot_rank)[:, None] == jnp.arange(slot_count, dtype=jnp.int32)[None, :]
    ).astype(BF16)
    over_rows = ((0,), (0,))

    def exchange(slots):
        parted = slots.reshape(owners, CAP, *slots.shape[1:])
        moved = lax.all_to_all(parted, "expert", split_axis=0, concat_axis=0, tiled=True)
        return moved.reshape(slots.shape)

    slot_rows = exchange(dot(placement, descriptors, over_rows).astype(BF16))
    slot_cot = exchange(dot(placement, cotangent, over_rows).astype(BF16)).astype(F32)
    weight, readout = w1[0], w2[0].astype(F32)
    preact = dot(slot_rows, weight)
    sig = jax.nn.sigmoid(preact)
    activated = preact * sig
    energy = jnp.sum(activated * readout, axis=1).astype(BF16)
    hidden_grad = (slot_cot[:, None] * readout * sig * (1.0 + preact * (1.0 - sig))).astype(BF16)
    input_grad = dot(hidden_grad, weight, ((1,), (1,))).astype(BF16)
    energies = dot(placement, exchange(energy)).astype(BF16)
    descriptor_grad = dot(placement, exchange(input_grad)).astype(BF16)
    w2_grad = lax.psum(jnp.sum(slot_cot[:, None] * activated, axis=0), "rep")
    w1_grad = lax.psum_scatter(
        dot(hidden_grad, slot_rows, over_rows).astype(BF16), "rep", scatter_dimension=0, tiled=True
    )
    return energies, descriptor_grad, w1_grad[None], w2_grad[None]


def on_device(descriptors, *rest):
    few = descriptors.shape[0] * lax.axis_size("expert") <= PLANE_ROWS
    return (by_blocks if few else by_slots)(descriptors, *rest)


def solution(mesh):
    in_specs = (
        P(("expert", "rep"), None),
        P(("expert", "rep"), None),
        P(("expert", "rep")),
        P("expert", None, None),
        P("expert", None),
    )
    out_specs = (
        P(("expert", "rep")),
        P(("expert", "rep"), None),
        P("expert", "rep", None),
        P("expert", None),
    )
    return jax.shard_map(
        on_device, mesh=mesh, in_specs=in_specs, out_specs=out_specs, check_vma=False
    )
```

```python
import functools

import jax
import jax.numpy as jnp
from jax import lax
from jax.experimental import pallas as pl
from jax.experimental.pallas import tpu as pltpu
from jax.sharding import PartitionSpec as P

CAP = 12
CROSSED_CHIPS = 0b1100
CROSSED_REPLICAS = 0b100
LANES = 128
PLANE_ROWS = 512
WAIT = 5_000_000_000
F32, BF16 = jnp.float32, jnp.bfloat16
VMEM = pl.BlockSpec(memory_space=pltpu.VMEM)
SMEM = pl.BlockSpec(memory_space=pltpu.SMEM)
HBM = pl.BlockSpec(memory_space=pltpu.HBM)
DMA = pltpu.SemaphoreType.DMA


def call(kernel, out_shape, operands, scratch=(), flops=0, scalars=0, hbm_outs=0):
    outs = jax.tree.leaves(out_shape)
    specs = [HBM] * hbm_outs + [VMEM] * (len(outs) - hbm_outs)
    moved = sum(x.size * x.dtype.itemsize for x in jax.tree.leaves((out_shape, operands)))
    return pl.pallas_call(
        kernel,
        out_shape=out_shape,
        in_specs=[SMEM] * scalars + [VMEM] * (len(operands) - scalars),
        out_specs=jax.tree.unflatten(jax.tree.structure(out_shape), specs),
        scratch_shapes=list(scratch),
        cost_estimate=pl.CostEstimate(flops=flops, bytes_accessed=moved, transcendentals=0),
        compiler_params=pltpu.CompilerParams(vmem_limit_bytes=24 << 20),
    )(*operands)


def swap(x, axis, k):
    return lax.ppermute(x, axis, [(i, i ^ k) for i in range(lax.axis_size(axis))])


def iota(shape, dim):
    return lax.broadcasted_iota(jnp.int32, shape, dim)


def dot(a, b, dims=((1,), (0,))):
    return lax.dot_general(a, b, (dims, ((), ())), preferred_element_type=F32)


def begin(where_ref, token_ref):
    token_ref[...] = jnp.zeros(token_ref.shape, F32)


def label_rows(rows_ref, ids_ref, cot_ref, after_ref, out_ref):
    rows, width = rows_ref.shape
    i, j = iota((rows, rows), 0), iota((rows, rows), 1)

    def column(square):
        return jnp.sum(square, axis=1, keepdims=True)

    ids_line = jnp.broadcast_to(ids_ref[...].astype(F32), (rows, rows))
    cot_line = jnp.broadcast_to(cot_ref[...].astype(F32), (rows, rows))
    ids = column(jnp.where(i == j, ids_line, 0.0))
    cot = column(jnp.where(i == j, cot_line, 0.0))
    rank = column(jnp.where((j < i) & (ids_line == ids), 1.0, 0.0))
    for k in range(width // LANES):
        out_ref[k * rows:(k + 1) * rows, :] = rows_ref[:, k * LANES:(k + 1) * LANES]
    lane, groups = iota((8, LANES), 1), rows // 8
    tags = jnp.zeros((8, LANES), F32)
    for field, values in enumerate((cot, ids, rank)):
        for k in range(groups):
            tags = jnp.where(lane == field * groups + k, values[8 * k:8 * (k + 1), :], tags)
    out_ref[width // LANES * rows:, :] = tags.astype(BF16)


def stack_blocks(*refs):
    blocks, out_ref = refs[:-1], refs[-1]
    size = blocks[0].shape[0] - 8
    for k, block in enumerate(blocks):
        out_ref[k * size:(k + 1) * size, :] = block[:size, :]
    tags = jnp.concatenate([block[size:, :].astype(F32) for block in blocks], axis=0)
    out_ref[len(blocks) * size:, :] = tags.astype(BF16)


def unstack_blocks(rows, stacks, xs):
    width = xs.shape[1] - LANES
    tiles, groups = width // LANES, rows // 8
    tags, at = [], 0
    for stack in stacks:
        blocks = stack.shape[0] // (tiles * rows + 8)
        for b in range(blocks):
            for k in range(tiles):
                first = (b * tiles + k) * rows
                xs[at:at + rows, k * LANES:(k + 1) * LANES] = stack[first:first + rows, :]
            at += rows
        tags.append(stack[blocks * tiles * rows:, :].astype(F32))
    total = xs.shape[0]
    tags = jnp.concatenate([
        part[8 * b:8 * (b + 1), :] for part in tags for b in range(part.shape[0] // 8) for _ in range(groups)
    ], axis=0)
    lane, row = iota((total, LANES), 1), iota((total, LANES), 0)
    group = (row >> 3) & (groups - 1)

    def column(field):
        return jnp.sum(jnp.where(lane == field * groups + group, tags, 0.0), axis=1, keepdims=True)

    xs[:, width:] = jnp.where(lane == 0, column(0), 0.0).astype(BF16)
    return column(1).astype(jnp.int32), column(2).astype(jnp.int32)


def gate(preact):
    sig = 0.5 * jnp.tanh(0.5 * preact) + 0.5
    return sig, preact * sig


def first_slot(total, rows):
    return (iota((total, 1), 0) >> rows.bit_length() - 1) * CAP


def partner_and_side(apart):
    return apart >> 1, (apart & 1) ^ (CROSSED_CHIPS >> (apart >> 1) & 1)


def one_hot(slot, size):
    return jnp.where(slot == iota((slot.shape[0], size), 1), 1.0, 0.0).astype(BF16)


def own_plane(
    chips, rows, where_ref, near_ref, other_ref, w1_ref, w2_ref, after_ref,
    keep_ref, give_ref, band_ref, kept_ref, readout_ref, spread_ref, xs, hs,
):
    width, hidden = w1_ref.shape
    band = band_ref.shape[1]
    half = chips * rows
    kept = 2 * chips * CAP
    ids, ranks = unstack_blocks(rows, (near_ref, other_ref), xs)
    slot = jnp.where(ids == where_ref[0], first_slot(2 * half, rows) + ranks, -1)
    apart = ids[:rows] ^ where_ref[0]
    chip, side = partner_and_side(apart)
    spread_ref[...] = one_hot(chip * (2 * CAP) + side * CAP + ranks[:rows], kept)
    kept_ref[...] = dot(one_hot(slot, kept), xs[...], ((0,), (0,))).astype(BF16)
    cot = kept_ref[:, width:].astype(F32)[:, 0:1]
    energy = jnp.zeros((kept, 1), F32)
    for c in range(0, hidden, band):
        part = slice(c, c + band)
        preact = dot(kept_ref[:, :width], w1_ref[:, part])
        sig, act = gate(preact)
        w2 = w2_ref[:, part].astype(F32)
        energy += jnp.sum(act * w2, axis=1, keepdims=True)
        hs[:, part] = (cot * w2 * sig * (1.0 + preact * (1.0 - sig))).astype(BF16)
        readout_ref[:, part] = jnp.sum(cot * act, axis=0, keepdims=True)
    band_ref[...] = hs[:, pl.ds(pl.multiple_of(where_ref[1] * band, band), band)]
    back = dot(hs[...], w1_ref[...], ((1,), (1,)))
    tail = jnp.where(iota((kept, LANES), 1) == 0, energy, 0.0)
    for out_ref, part in ((keep_ref, slice(0, kept // 2)), (give_ref, slice(kept // 2, kept))):
        out_ref[:, :width] = back[part, :].astype(BF16)
        out_ref[:, width:] = tail[part, :].astype(BF16)


def pack_slots(slots, out_ref):
    size, width = slots.shape[0], slots.shape[1] - LANES
    for t in range(width // LANES):
        out_ref[t * size:(t + 1) * size, :] = slots[:, t * LANES:(t + 1) * LANES].astype(BF16)
    lane, behind = iota((8, LANES), 1), jnp.zeros((8, LANES), F32)
    for g in range(size // 8):
        behind = jnp.where(lane == g, slots[8 * g:8 * (g + 1), width:width + 1], behind)
    out_ref[width // LANES * size:, :] = behind.astype(BF16)


def unpack_slots(packed_ref, ys, at):
    tiles = ys.shape[1] // LANES - 1
    size = (packed_ref.shape[0] - 8) // tiles
    for t in range(tiles):
        ys[at:at + size, t * LANES:(t + 1) * LANES] = packed_ref[t * size:(t + 1) * size, :]
    behind = jnp.concatenate([packed_ref[tiles * size:, :].astype(F32)] * (size // 8), axis=0)
    own_lane = iota((size, LANES), 1) == iota((size, LANES), 0) >> 3
    ys[at:at + size, tiles * LANES:] = jnp.where(own_lane, behind, 0.0).astype(BF16)
    return at + size


def join_cores(keep_ref, got_ref, *outs):
    keep, got = keep_ref[...].astype(F32), got_ref[...].astype(F32)
    for k, out_ref in enumerate(outs):
        part = slice(CAP * k, CAP * (k + 1))
        pack_slots(jnp.concatenate([keep[part, :], got[part, :]], axis=0), out_ref)


def pick_slots(rows, where_ref, far_ref, other_ref, *refs):
    outs, xs = refs[:-1], refs[-1]
    size = (outs[0].shape[0] - 8) // (xs.shape[1] // LANES - 1)
    ids, ranks = unstack_blocks(rows, (far_ref, other_ref), xs)
    apart = ids ^ where_ref[0]
    chip, side = partner_and_side(apart)
    slot = jnp.where(side == 0, chip * size + first_slot(xs.shape[0], rows) + ranks, -1)
    picked = dot(one_hot(slot, len(outs) * size), xs[...], ((0,), (0,)))
    for k, out_ref in enumerate(outs):
        pack_slots(picked[k * size:(k + 1) * size, :], out_ref)


def place_rows(n, spread_ref, w2_grad_ref, *refs):
    slots, (w2_grad_hbm, grad_ref, energy_ref, ys, sem) = refs[:n], refs[n:]
    copy = pltpu.make_async_copy(w2_grad_ref, w2_grad_hbm, sem)
    copy.start()
    width = grad_ref.shape[1]
    at = 0
    for slot in slots:
        at = unpack_slots(slot, ys, at)
    grad_ref[...] = dot(spread_ref[...], ys[:, :width]).astype(BF16)
    energy = dot(ys[:, width:], spread_ref[...], ((0,), (1,)))[:8, :]
    energy_ref[...] = jnp.sum(energy, axis=0, keepdims=True).astype(BF16)
    copy.wait()


def all_replicas(n, where_ref, *refs):
    slots = refs[:n]
    kept_ref, w1_ref, w2_ref, band_ref, readout_ref, w1_grad_hbm, w2_grad_ref = refs[n:n + 7]
    ys, hs, w1_grad_ref, sem = refs[n + 7:]
    width, hidden = w1_ref.shape
    band = band_ref.shape[1]
    new = 0
    for slot in slots:
        new = unpack_slots(slot, ys, new)
    ys[new:, :] = kept_ref[...]
    hs[new:, :] = band_ref[...]
    cot = jnp.sum(ys[:new, width:].astype(F32), axis=1, keepdims=True)
    bands = hidden // band
    for j in range(bands):
        at = where_ref[1] + j
        at = jnp.where(at >= bands, at - bands, at)
        part = pl.ds(pl.multiple_of(at * band, band), band)
        preact = dot(ys[:new, :width], w1_ref[:, part])
        sig, act = gate(preact)
        w2_grad_ref[:, part] = readout_ref[:, part] + jnp.sum(cot * act, axis=0, keepdims=True)
        if j == 0:
            w2 = w2_ref[:, part].astype(F32)
            hs[:new, :] = (cot * w2 * sig * (1.0 + preact * (1.0 - sig))).astype(BF16)
            w1_grad_ref[...] = dot(hs[...], ys[:, :width], ((0,), (0,))).astype(BF16)
            copy = pltpu.make_async_copy(w1_grad_ref, w1_grad_hbm, sem)
            copy.start()
    copy.wait()


def by_blocks(descriptors, expert_ids, cotangent, w1, w2):
    owners, replicas = lax.axis_size("expert"), lax.axis_size("rep")
    rows, width = descriptors.shape
    wide = width + LANES
    hidden = w1.shape[2]
    band = hidden // replicas
    chips = owners // 2
    kept = owners * CAP
    where = jnp.stack([lax.axis_index("expert"), lax.axis_index("rep")]).astype(jnp.int32)

    def shape(*dims, dtype=BF16):
        return jax.ShapeDtypeStruct(dims, dtype)

    def to_chips(blocks):
        return [blocks[0]] + [swap(blocks[k], "expert", 2 * k + (CROSSED_CHIPS >> k & 1)) for k in range(1, chips)]

    begun = call(begin, shape(1, LANES, dtype=F32), (where,), flops=WAIT, scalars=1)
    length = width // LANES * rows + 8
    own = call(
        label_rows, shape(length, LANES),
        (descriptors, expert_ids.reshape(1, rows), cotangent.reshape(1, rows), begun),
    )
    readout = w2
    weight = w1[0]
    far = [swap(own, ("expert", "rep"), replicas * (CROSSED_REPLICAS >> k & 1) + k) for k in range(1, replicas)]
    far = call(stack_blocks, shape(len(far) * length, LANES), tuple(far), flops=WAIT)
    far_other = swap(far, "expert", 1)
    near = to_chips([own] * chips)
    near = call(stack_blocks, shape(chips * length, LANES), tuple(near), flops=WAIT)
    near_other = swap(near, "expert", 1)

    size = 2 * (replicas - 1) * CAP
    chosen = call(
        functools.partial(pick_slots, rows), [shape(width // LANES * size + 8, LANES)] * chips, (where, far, far_other),
        (pltpu.VMEM((2 * (replicas - 1) * rows, wide), BF16),),
        flops=WAIT, scalars=1,
    )
    slots = to_chips(chosen)

    keep, give, band_grad, kept_rows, readout_part, spread = call(
        functools.partial(own_plane, chips, rows),
        [
            shape(kept // 2, wide), shape(kept // 2, wide), shape(kept, band), shape(kept, wide),
            shape(1, hidden, dtype=F32), shape(rows, kept),
        ],
        (where, near, near_other, weight, readout, chosen[0]),
        (pltpu.VMEM((owners * rows, wide), BF16), pltpu.VMEM((kept, hidden), BF16)),
        flops=4 * kept * width * hidden, scalars=1,
    )
    got = swap(give, "expert", 1)
    back = to_chips(call(join_cores, [shape(width // LANES * 2 * CAP + 8, LANES)] * chips, (keep, got)))

    w1_grad, w2_grad = call(
        functools.partial(all_replicas, chips),
        (shape(band, width), shape(1, hidden, dtype=F32)),
        (where, *slots, kept_rows, weight, readout, band_grad, readout_part),
        (
            pltpu.VMEM((chips * size + kept, wide), BF16), pltpu.VMEM((chips * size + kept, band), BF16),
            pltpu.VMEM((band, width), BF16), DMA,
        ),
        flops=4 * WAIT, scalars=1, hbm_outs=1,
    )

    w2_grad, descriptor_grad, energies = call(
        functools.partial(place_rows, chips),
        (shape(1, hidden, dtype=F32), shape(rows, width), shape(1, rows)),
        (spread, w2_grad, *back), (pltpu.VMEM((kept, wide), BF16), DMA), hbm_outs=1,
    )
    return energies.reshape(rows), descriptor_grad, w1_grad[None], w2_grad


def by_slots(descriptors, expert_ids, cotangent, w1, w2):
    owners = lax.axis_size("expert")
    columns = descriptors.shape[1]
    slot_count = owners * CAP
    targets = expert_ids[:, 0]
    member = (targets[:, None] == jnp.arange(owners, dtype=jnp.int32)[None, :]).astype(jnp.int32)
    slot_rank = jnp.sum((jnp.cumsum(member, axis=0) - 1) * member, axis=1)
    placement = (
        (targets * CAP + slot_rank)[:, None] == jnp.arange(slot_count, dtype=jnp.int32)[None, :]
    ).astype(BF16)
    over_rows = ((0,), (0,))

    def exchange(slots):
        parted = slots.reshape(owners, CAP, *slots.shape[1:])
        moved = lax.all_to_all(parted, "expert", split_axis=0, concat_axis=0, tiled=True)
        return moved.reshape(slots.shape)

    slot_rows = exchange(dot(placement, descriptors, over_rows).astype(BF16))
    slot_cot = exchange(dot(placement, cotangent, over_rows).astype(BF16)).astype(F32)
    weight, readout = w1[0], w2[0].astype(F32)
    preact = dot(slot_rows, weight)
    sig = jax.nn.sigmoid(preact)
    activated = preact * sig
    energy = jnp.sum(activated * readout, axis=1).astype(BF16)
    hidden_grad = (slot_cot[:, None] * readout * sig * (1.0 + preact * (1.0 - sig))).astype(BF16)
    input_grad = dot(hidden_grad, weight, ((1,), (1,))).astype(BF16)
    energies = dot(placement, exchange(energy)).astype(BF16)
    descriptor_grad = dot(placement, exchange(input_grad)).astype(BF16)
    w2_grad = lax.psum(jnp.sum(slot_cot[:, None] * activated, axis=0), "rep")
    w1_grad = lax.psum_scatter(
        dot(hidden_grad, slot_rows, over_rows).astype(BF16), "rep", scatter_dimension=0, tiled=True
    )
    return energies, descriptor_grad, w1_grad[None], w2_grad[None]


def on_device(descriptors, *rest):
    few = descriptors.shape[0] * lax.axis_size("expert") <= PLANE_ROWS
    return (by_blocks if few else by_slots)(descriptors, *rest)


def solution(mesh):
    in_specs = (
        P(("expert", "rep"), None),
        P(("expert", "rep"), None),
        P(("expert", "rep")),
        P("expert", None, None),
        P("expert", None),
    )
    out_specs = (
        P(("expert", "rep")),
        P(("expert", "rep"), None),
        P("expert", "rep", None),
        P("expert", None),
    )
    return jax.shard_map(
        on_device, mesh=mesh, in_specs=in_specs, out_specs=out_specs, check_vma=False
    )
```

```python
import functools

import jax
import jax.numpy as jnp
from jax import lax
from jax.experimental import pallas as pl
from jax.experimental.pallas import tpu as pltpu
from jax.sharding import PartitionSpec as P

CAP = 12
CROSSED_CHIPS = 0b1100
CROSSED_REPLICAS = 0b100
LANES = 128
PLANE_ROWS = 512
WAIT = 5_000_000_000
F32, BF16 = jnp.float32, jnp.bfloat16
VMEM = pl.BlockSpec(memory_space=pltpu.VMEM)
SMEM = pl.BlockSpec(memory_space=pltpu.SMEM)
HBM = pl.BlockSpec(memory_space=pltpu.HBM)
DMA = pltpu.SemaphoreType.DMA


def call(kernel, out_shape, operands, scratch=(), flops=0, scalars=0, hbm_outs=0):
    outs = jax.tree.leaves(out_shape)
    specs = [HBM] * hbm_outs + [VMEM] * (len(outs) - hbm_outs)
    moved = sum(x.size * x.dtype.itemsize for x in jax.tree.leaves((out_shape, operands)))
    return pl.pallas_call(
        kernel,
        out_shape=out_shape,
        in_specs=[SMEM] * scalars + [VMEM] * (len(operands) - scalars),
        out_specs=jax.tree.unflatten(jax.tree.structure(out_shape), specs),
        scratch_shapes=list(scratch),
        cost_estimate=pl.CostEstimate(flops=flops, bytes_accessed=moved, transcendentals=0),
        compiler_params=pltpu.CompilerParams(vmem_limit_bytes=24 << 20),
    )(*operands)


def swap(x, axis, k):
    return lax.ppermute(x, axis, [(i, i ^ k) for i in range(lax.axis_size(axis))])


def iota(shape, dim):
    return lax.broadcasted_iota(jnp.int32, shape, dim)


def dot(a, b, dims=((1,), (0,))):
    return lax.dot_general(a, b, (dims, ((), ())), preferred_element_type=F32)


def begin(where_ref, token_ref):
    token_ref[...] = jnp.zeros(token_ref.shape, F32)


def label_rows(rows_ref, ids_ref, cot_ref, after_ref, out_ref):
    rows, width = rows_ref.shape
    i, j = iota((rows, rows), 0), iota((rows, rows), 1)

    def column(square):
        return jnp.sum(square, axis=1, keepdims=True)

    ids_line = jnp.broadcast_to(ids_ref[...].astype(F32), (rows, rows))
    cot_line = jnp.broadcast_to(cot_ref[...].astype(F32), (rows, rows))
    ids = column(jnp.where(i == j, ids_line, 0.0))
    cot = column(jnp.where(i == j, cot_line, 0.0))
    rank = column(jnp.where((j < i) & (ids_line == ids), 1.0, 0.0))
    for k in range(width // LANES):
        out_ref[k * rows:(k + 1) * rows, :] = rows_ref[:, k * LANES:(k + 1) * LANES]
    lane, groups = iota((8, LANES), 1), rows // 8
    tags = jnp.zeros((8, LANES), F32)
    for field, values in enumerate((cot, ids, rank)):
        for k in range(groups):
            tags = jnp.where(lane == field * groups + k, values[8 * k:8 * (k + 1), :], tags)
    out_ref[width // LANES * rows:, :] = tags.astype(BF16)


def stack_blocks(*refs):
    blocks, out_ref = refs[:-1], refs[-1]
    size = blocks[0].shape[0] - 8
    for k, block in enumerate(blocks):
        out_ref[k * size:(k + 1) * size, :] = block[:size, :]
    tags = jnp.concatenate([block[size:, :].astype(F32) for block in blocks], axis=0)
    out_ref[len(blocks) * size:, :] = tags.astype(BF16)


def unstack_blocks(rows, stacks, xs):
    width = xs.shape[1] - LANES
    tiles, groups = width // LANES, rows // 8
    tags, at = [], 0
    for stack in stacks:
        blocks = stack.shape[0] // (tiles * rows + 8)
        for b in range(blocks):
            for k in range(tiles):
                first = (b * tiles + k) * rows
                xs[at:at + rows, k * LANES:(k + 1) * LANES] = stack[first:first + rows, :]
            at += rows
        tags.append(stack[blocks * tiles * rows:, :].astype(F32))
    total = xs.shape[0]
    tags = jnp.concatenate([
        part[8 * b:8 * (b + 1), :] for part in tags for b in range(part.shape[0] // 8) for _ in range(groups)
    ], axis=0)
    lane, row = iota((total, LANES), 1), iota((total, LANES), 0)
    group = (row >> 3) & (groups - 1)

    def column(field):
        return jnp.sum(jnp.where(lane == field * groups + group, tags, 0.0), axis=1, keepdims=True)

    xs[:, width:] = jnp.where(lane == 0, column(0), 0.0).astype(BF16)
    return column(1).astype(jnp.int32), column(2).astype(jnp.int32)


def gate(preact):
    sig = 0.5 * jnp.tanh(0.5 * preact) + 0.5
    return sig, preact * sig


def first_slot(total, rows):
    return (iota((total, 1), 0) >> rows.bit_length() - 1) * CAP


def partner_and_side(apart):
    return apart >> 1, (apart & 1) ^ (CROSSED_CHIPS >> (apart >> 1) & 1)


def one_hot(slot, size):
    return jnp.where(slot == iota((slot.shape[0], size), 1), 1.0, 0.0).astype(BF16)


def own_plane(
    chips, rows, where_ref, near_ref, other_ref, w1_ref, w2_ref, after_ref,
    keep_ref, give_ref, band_ref, kept_ref, readout_ref, spread_ref, xs, hs,
):
    width, hidden = w1_ref.shape
    band = band_ref.shape[1]
    half = chips * rows
    kept = 2 * chips * CAP
    ids, ranks = unstack_blocks(rows, (near_ref, other_ref), xs)
    slot = jnp.where(ids == where_ref[0], first_slot(2 * half, rows) + ranks, -1)
    apart = ids[:rows] ^ where_ref[0]
    chip, side = partner_and_side(apart)
    spread_ref[...] = one_hot(chip * (2 * CAP) + side * CAP + ranks[:rows], kept)
    kept_ref[...] = dot(one_hot(slot, kept), xs[...], ((0,), (0,))).astype(BF16)
    cot = kept_ref[:, width:].astype(F32)[:, 0:1]
    energy = jnp.zeros((kept, 1), F32)
    for c in range(0, hidden, band):
        part = slice(c, c + band)
        preact = dot(kept_ref[:, :width], w1_ref[:, part])
        sig, act = gate(preact)
        w2 = w2_ref[:, part].astype(F32)
        energy += jnp.sum(act * w2, axis=1, keepdims=True)
        hs[:, part] = (cot * w2 * sig * (1.0 + preact * (1.0 - sig))).astype(BF16)
        readout_ref[:, part] = jnp.sum(cot * act, axis=0, keepdims=True)
    band_ref[...] = hs[:, pl.ds(pl.multiple_of(where_ref[1] * band, band), band)]
    back = dot(hs[...], w1_ref[...], ((1,), (1,)))
    tail = jnp.where(iota((kept, LANES), 1) == 0, energy, 0.0)
    for out_ref, part in ((keep_ref, slice(0, kept // 2)), (give_ref, slice(kept // 2, kept))):
        out_ref[:, :width] = back[part, :].astype(BF16)
        out_ref[:, width:] = tail[part, :].astype(BF16)


def pack_slots(slots, out_ref):
    size, width = slots.shape[0], slots.shape[1] - LANES
    for t in range(width // LANES):
        out_ref[t * size:(t + 1) * size, :] = slots[:, t * LANES:(t + 1) * LANES].astype(BF16)
    lane, behind = iota((8, LANES), 1), jnp.zeros((8, LANES), F32)
    for g in range(size // 8):
        behind = jnp.where(lane == g, slots[8 * g:8 * (g + 1), width:width + 1], behind)
    out_ref[width // LANES * size:, :] = behind.astype(BF16)


def unpack_slots(packed_ref, ys, at):
    tiles = ys.shape[1] // LANES - 1
    size = (packed_ref.shape[0] - 8) // tiles
    for t in range(tiles):
        ys[at:at + size, t * LANES:(t + 1) * LANES] = packed_ref[t * size:(t + 1) * size, :]
    behind = jnp.concatenate([packed_ref[tiles * size:, :].astype(F32)] * (size // 8), axis=0)
    own_lane = iota((size, LANES), 1) == iota((size, LANES), 0) >> 3
    ys[at:at + size, tiles * LANES:] = jnp.where(own_lane, behind, 0.0).astype(BF16)
    return at + size


def join_cores(keep_ref, got_ref, *outs):
    keep, got = keep_ref[...].astype(F32), got_ref[...].astype(F32)
    for k, out_ref in enumerate(outs):
        part = slice(CAP * k, CAP * (k + 1))
        pack_slots(jnp.concatenate([keep[part, :], got[part, :]], axis=0), out_ref)


def pick_slots(rows, start, count, where_ref, far_ref, other_ref, *refs):
    outs, xs = refs[-1 - count:-1], refs[-1]
    size = (outs[0].shape[0] - 8) // (xs.shape[1] // LANES - 1)
    ids, ranks = unstack_blocks(rows, (far_ref, other_ref), xs)
    apart = ids ^ where_ref[0]
    chip, side = partner_and_side(apart)
    slot = jnp.where(side == 0, (chip - start) * size + first_slot(xs.shape[0], rows) + ranks, -1)
    picked = dot(one_hot(slot, len(outs) * size), xs[...], ((0,), (0,)))
    for k, out_ref in enumerate(outs):
        pack_slots(picked[k * size:(k + 1) * size, :], out_ref)


def place_rows(n, spread_ref, w2_grad_ref, *refs):
    slots, (w2_grad_hbm, grad_ref, energy_ref, ys, sem) = refs[:n], refs[n:]
    copy = pltpu.make_async_copy(w2_grad_ref, w2_grad_hbm, sem)
    copy.start()
    width = grad_ref.shape[1]
    at = 0
    for slot in slots:
        at = unpack_slots(slot, ys, at)
    grad_ref[...] = dot(spread_ref[...], ys[:, :width]).astype(BF16)
    energy = dot(ys[:, width:], spread_ref[...], ((0,), (1,)))[:8, :]
    energy_ref[...] = jnp.sum(energy, axis=0, keepdims=True).astype(BF16)
    copy.wait()


def all_replicas(n, where_ref, *refs):
    slots = refs[:n]
    kept_ref, w1_ref, w2_ref, band_ref, readout_ref, w1_grad_hbm, w2_grad_ref = refs[n:n + 7]
    ys, hs, w1_grad_ref, sem = refs[n + 7:]
    width, hidden = w1_ref.shape
    band = band_ref.shape[1]
    new = 0
    for slot in slots:
        new = unpack_slots(slot, ys, new)
    ys[new:, :] = kept_ref[...]
    hs[new:, :] = band_ref[...]
    cot = jnp.sum(ys[:new, width:].astype(F32), axis=1, keepdims=True)
    bands = hidden // band
    for j in range(bands):
        at = where_ref[1] + j
        at = jnp.where(at >= bands, at - bands, at)
        part = pl.ds(pl.multiple_of(at * band, band), band)
        preact = dot(ys[:new, :width], w1_ref[:, part])
        sig, act = gate(preact)
        w2_grad_ref[:, part] = readout_ref[:, part] + jnp.sum(cot * act, axis=0, keepdims=True)
        if j == 0:
            w2 = w2_ref[:, part].astype(F32)
            hs[:new, :] = (cot * w2 * sig * (1.0 + preact * (1.0 - sig))).astype(BF16)
            w1_grad_ref[...] = dot(hs[...], ys[:, :width], ((0,), (0,))).astype(BF16)
            copy = pltpu.make_async_copy(w1_grad_ref, w1_grad_hbm, sem)
            copy.start()
    copy.wait()


def by_blocks(descriptors, expert_ids, cotangent, w1, w2):
    owners, replicas = lax.axis_size("expert"), lax.axis_size("rep")
    rows, width = descriptors.shape
    wide = width + LANES
    hidden = w1.shape[2]
    band = hidden // replicas
    chips = owners // 2
    kept = owners * CAP
    where = jnp.stack([lax.axis_index("expert"), lax.axis_index("rep")]).astype(jnp.int32)

    def shape(*dims, dtype=BF16):
        return jax.ShapeDtypeStruct(dims, dtype)

    def to_chips(blocks):
        return [blocks[0]] + [swap(blocks[k], "expert", 2 * k + (CROSSED_CHIPS >> k & 1)) for k in range(1, chips)]

    begun = call(begin, shape(1, LANES, dtype=F32), (where,), flops=WAIT, scalars=1)
    length = width // LANES * rows + 8
    own = call(
        label_rows, shape(length, LANES),
        (descriptors, expert_ids.reshape(1, rows), cotangent.reshape(1, rows), begun),
    )
    readout = w2
    weight = w1[0]
    far = [swap(own, ("expert", "rep"), replicas * (CROSSED_REPLICAS >> k & 1) + k) for k in range(1, replicas)]
    far = call(stack_blocks, shape(len(far) * length, LANES), tuple(far), flops=WAIT)
    far_other = swap(far, "expert", 1)
    near = to_chips([own] * chips)
    near = call(stack_blocks, shape(chips * length, LANES), tuple(near), flops=WAIT)
    near_other = swap(near, "expert", 1)

    size = 2 * (replicas - 1) * CAP
    def pick(start, count, *after):
        return call(
            functools.partial(pick_slots, rows, start, count), [shape(width // LANES * size + 8, LANES)] * count,
            (where, far, far_other, *after),
            (pltpu.VMEM((2 * (replicas - 1) * rows, wide), BF16),), flops=WAIT, scalars=1,
        )

    chosen = pick(1, chips - 1)
    slots = to_chips([chosen[0], *chosen])[1:]

    keep, give, band_grad, kept_rows, readout_part, spread = call(
        functools.partial(own_plane, chips, rows),
        [
            shape(kept // 2, wide), shape(kept // 2, wide), shape(kept, band), shape(kept, wide),
            shape(1, hidden, dtype=F32), shape(rows, kept),
        ],
        (where, near, near_other, weight, readout, chosen[0]),
        (pltpu.VMEM((owners * rows, wide), BF16), pltpu.VMEM((kept, hidden), BF16)),
        flops=4 * kept * width * hidden, scalars=1,
    )
    got = swap(give, "expert", 1)
    slots = [*pick(0, 1, band_grad), *slots]
    back = to_chips(call(join_cores, [shape(width // LANES * 2 * CAP + 8, LANES)] * chips, (keep, got)))

    w1_grad, w2_grad = call(
        functools.partial(all_replicas, chips),
        (shape(band, width), shape(1, hidden, dtype=F32)),
        (where, *slots, kept_rows, weight, readout, band_grad, readout_part),
        (
            pltpu.VMEM((chips * size + kept, wide), BF16), pltpu.VMEM((chips * size + kept, band), BF16),
            pltpu.VMEM((band, width), BF16), DMA,
        ),
        flops=4 * WAIT, scalars=1, hbm_outs=1,
    )

    w2_grad, descriptor_grad, energies = call(
        functools.partial(place_rows, chips),
        (shape(1, hidden, dtype=F32), shape(rows, width), shape(1, rows)),
        (spread, w2_grad, *back), (pltpu.VMEM((kept, wide), BF16), DMA), hbm_outs=1,
    )
    return energies.reshape(rows), descriptor_grad, w1_grad[None], w2_grad


def by_slots(descriptors, expert_ids, cotangent, w1, w2):
    owners = lax.axis_size("expert")
    columns = descriptors.shape[1]
    slot_count = owners * CAP
    targets = expert_ids[:, 0]
    member = (targets[:, None] == jnp.arange(owners, dtype=jnp.int32)[None, :]).astype(jnp.int32)
    slot_rank = jnp.sum((jnp.cumsum(member, axis=0) - 1) * member, axis=1)
    placement = (
        (targets * CAP + slot_rank)[:, None] == jnp.arange(slot_count, dtype=jnp.int32)[None, :]
    ).astype(BF16)
    over_rows = ((0,), (0,))

    def exchange(slots):
        parted = slots.reshape(owners, CAP, *slots.shape[1:])
        moved = lax.all_to_all(parted, "expert", split_axis=0, concat_axis=0, tiled=True)
        return moved.reshape(slots.shape)

    slot_rows = exchange(dot(placement, descriptors, over_rows).astype(BF16))
    slot_cot = exchange(dot(placement, cotangent, over_rows).astype(BF16)).astype(F32)
    weight, readout = w1[0], w2[0].astype(F32)
    preact = dot(slot_rows, weight)
    sig = jax.nn.sigmoid(preact)
    activated = preact * sig
    energy = jnp.sum(activated * readout, axis=1).astype(BF16)
    hidden_grad = (slot_cot[:, None] * readout * sig * (1.0 + preact * (1.0 - sig))).astype(BF16)
    input_grad = dot(hidden_grad, weight, ((1,), (1,))).astype(BF16)
    energies = dot(placement, exchange(energy)).astype(BF16)
    descriptor_grad = dot(placement, exchange(input_grad)).astype(BF16)
    w2_grad = lax.psum(jnp.sum(slot_cot[:, None] * activated, axis=0), "rep")
    w1_grad = lax.psum_scatter(
        dot(hidden_grad, slot_rows, over_rows).astype(BF16), "rep", scatter_dimension=0, tiled=True
    )
    return energies, descriptor_grad, w1_grad[None], w2_grad[None]


def on_device(descriptors, *rest):
    few = descriptors.shape[0] * lax.axis_size("expert") <= PLANE_ROWS
    return (by_blocks if few else by_slots)(descriptors, *rest)


def solution(mesh):
    in_specs = (
        P(("expert", "rep"), None),
        P(("expert", "rep"), None),
        P(("expert", "rep")),
        P("expert", None, None),
        P("expert", None),
    )
    out_specs = (
        P(("expert", "rep")),
        P(("expert", "rep"), None),
        P("expert", "rep", None),
        P("expert", None),
    )
    return jax.shard_map(
        on_device, mesh=mesh, in_specs=in_specs, out_specs=out_specs, check_vma=False
    )
```
